256 devices in a mesh: freq: 32 (over z_lo, y, x), tile: 8 (over z_hi, core).
Axes of the slice: x: 4, y: 4, z: 8 (z_hi: 4, z_lo: 2; z = z_hi * 2 + z_lo), core: 2. Of those that a mesh axis runs over, the one named last changes fastest.
Arguments:
- response: bfloat16 [2, 128, 2048, 2048], P(None, 'freq', 'tile'), may hold values from -0.09375 to 0.09375
- direct: float32 [2, 128, 8, 2048], P(None, 'freq', None, 'tile'), may hold values from -6 to 6
- onset: int32 [8, 2048], P(None, 'tile'), may hold values from 32 to 223
Outputs:
- minus_spectrum: float32 [2, 128, 8, 2048], P(None, 'freq', None, 'tile')
- plus_spectrum: float32 [2, 128, 8, 2048], P(None, 'freq', None, 'tile')
The draws below stay inside these ranges and needn't reach their ends.
Inputs may be any that keep to these rules, and one draw needn't show every extreme that they name: onset sample of the direct arrival for each focal point and position.
All inputs are finite; a program needn't handle non-finite values.
Results may differ from the reference program's by a relative error of at most 0.0029.
Values may be sent and summed in bfloat16 or wider, within the bound.
No kernel may reach another device: no remote copies, remote signals or barrier semaphores. Data moves between devices by JAX's collectives and lax.ppermute only.
A program may use at most 64 MiB of HBM per device.

```python
import math
import jax
import jax.numpy as jnp
from jax import lax

N = 2048
NT = 512
FP = 8
ITERS = 2
FIRST_BIN = 16
NF = 128


def touch_ends(entries, key, smallest, largest):
    index_at = [jax.random.randint(jax.random.fold_in(key, axis), (), 0, length) for axis, length in enumerate(entries.shape)]
    main_axis = entries.shape.index(max(entries.shape))
    beside = index_at[:main_axis] + [(index_at[main_axis] + 1) % entries.shape[main_axis]] + index_at[main_axis + 1:]
    return entries.at[tuple(index_at)].set(smallest).at[tuple(beside)].set(largest)


def level_of(own_key, shape, split, low, top_value):
    factor_of, own = 1.0, jax.random.fold_in(own_key, 6)
    for position, blocks in split:
        draws = jnp.exp(jax.random.uniform(jax.random.fold_in(own, position), (blocks,), jnp.float32, low / len(split), top_value / len(split)))
        factor_of = factor_of * jnp.repeat(draws, shape[position] // blocks).reshape([-1 if axis == position else 1 for axis in range(len(shape))])
    return factor_of


def gaussian(stream_key, shape, deviation, most, split=(), held_as=jnp.bfloat16):
    loudness = level_of(stream_key, shape, split, -0.22, 0.18) if split else 1.0
    values = jax.random.normal(stream_key, shape, jnp.float32) * deviation * loudness
    return jnp.minimum(jnp.maximum(values, -most), most).astype(held_as)


def setup_inputs(seed: int = 0) -> dict:
    arg_keys = jax.random.split(jax.random.key(seed), 4)
    return {
        "response": gaussian(arg_keys[0], (2, NF, N, N), (2 * N) ** -0.5, 0.09375, ((1, 32), (2, 8))),
        "direct": gaussian(arg_keys[1], (2, NF, FP, N), 1.0, 6.0, ((1, 32), (3, 8)), jnp.float32),
        "onset": touch_ends(jax.random.randint(arg_keys[2], (FP, N), NT // 16, 7 * NT // 16), jax.random.fold_in(arg_keys[2], 1), NT // 16, (7 * NT // 16) - 1).astype(jnp.int32),
    }


def tables(bins, times):
    phase = bins[:, None] * times[None, :] % NT
    angle = 2.0 * math.pi / NT * phase.astype(jnp.float32)
    return (jnp.cos(angle), jnp.sin(angle))

def window_mask(onset, times):
    shifted = jnp.where(times >= NT // 2, times - NT, times)
    keep = (shifted[None, :, None] > -onset[:, None, :]) & (shifted[None, :, None] < onset[:, None, :])
    return keep.astype(jnp.float32)

def roundtrip(spectrum, onset):
    scale = math.sqrt(2.0 / NT)
    bins = FIRST_BIN + jnp.arange(NF, dtype=jnp.int32)
    times = jnp.arange(NT, dtype=jnp.int32)
    cosine, sine = tables(bins, times)
    highest = lax.Precision.HIGHEST
    signal = scale * (jnp.einsum('jt,jpn->ptn', cosine, spectrum[0], precision=highest) - jnp.einsum('jt,jpn->ptn', sine, spectrum[1], precision=highest))
    signal = signal * window_mask(onset, times)
    real = scale * jnp.einsum('jt,ptn->jpn', cosine, signal, precision=highest)
    imag = -scale * jnp.einsum('jt,ptn->jpn', sine, signal, precision=highest)
    return jnp.stack([real, imag])

def forward_product(response, vectors):
    dims = (((1,), (1,)), ((), ()))

    def single(item):
        rpart, ipart, vreal, vimag = item

        def product(left, right):
            return lax.dot_general(left, right, dims, preferred_element_type=jnp.float32)
        return jnp.stack([product(vreal, rpart) - product(vimag, ipart), product(vimag, rpart) + product(vreal, ipart)])
    result = lax.map(single, (response[0], response[1], vectors[0], vectors[1]))
    return jnp.transpose(result, (1, 0, 2, 3))

def adjoint_product(response, vectors):

    def single(item):
        rpart, ipart, vreal, vimag = item

        def product(left, right):
            return jnp.dot(left, right, preferred_element_type=jnp.float32)
        return jnp.stack([product(vreal, rpart) + product(vimag, ipart), product(vimag, rpart) - product(vreal, ipart)])
    result = lax.map(single, (response[0], response[1], vectors[0], vectors[1]))
    return jnp.transpose(result, (1, 0, 2, 3))

def reference(response, direct, onset):
    plus = direct
    minus = direct
    for step in range(ITERS):
        upgoing = forward_product(response, plus.astype(jnp.bfloat16))
        minus = roundtrip(upgoing, onset)
        sources = adjoint_product(response, minus.astype(jnp.bfloat16))
        plus = direct + roundtrip(sources, onset)
    return (minus, plus)
```

```python
import functools
import math

import jax
import jax.numpy as jnp
import numpy as np
from jax import lax
from jax.experimental import pallas as pl
from jax.experimental.pallas import tpu as pltpu
from jax.sharding import PartitionSpec as P

NT = 512
ITERS = 2
FIRST_BIN = 16
NF = 128
FP = 8
LAGS = 224
LANES = 128
BF16 = jnp.bfloat16
F32 = jnp.float32
VMEM_LIMIT = 24 * 1024 * 1024


def split(table):
    high = table.astype(np.float32).astype(jnp.bfloat16)
    low = (table - high.astype(np.float64)).astype(np.float32).astype(jnp.bfloat16)
    return high, low


def tables():
    bins = FIRST_BIN + np.arange(NF)
    lags = np.arange(LAGS)
    angle = 2.0 * math.pi / NT * ((lags[:, None] * bins[None, :]) % NT)
    weight = np.where(lags == 0, 2.0 / NT, 4.0 / NT)
    inverse, forward = [], []
    for table in (np.cos(angle), np.sin(angle)):
        high, low = split(table)
        inverse.append(np.concatenate([high, high, low], axis=1))
        high, low = split((table * weight[:, None]).T)
        forward.append(np.concatenate([high, high, low], axis=1))
    return np.stack(inverse), np.stack(forward)


def pieces(value):
    high = value.astype(BF16)
    low = (value - high.astype(F32)).astype(BF16)
    return jnp.concatenate([high, low, high], axis=0)


def roundtrip_kernel(summed, copies, place, inverse, forward, onset, blocks, out):
    if summed:
        rows = NF
        spectrum = blocks[:rows, :].astype(F32)
        for tile in range(1, blocks.shape[0] // rows):
            spectrum += blocks[tile * rows : (tile + 1) * rows, :].astype(F32)
    else:
        spectrum = blocks[...]
    signal = jnp.dot(inverse[0], pieces(spectrum), preferred_element_type=F32)
    focal = lax.broadcasted_iota(jnp.int32, onset.shape, 0)
    limit = jnp.sum(jnp.where(focal == place[1], onset[...], 0), axis=0, keepdims=True)
    lag = lax.broadcasted_iota(jnp.int32, signal.shape, 0)
    signal = jnp.where(lag < limit, signal, 0.0)
    result = jnp.dot(forward[0], pieces(signal), preferred_element_type=F32)
    result = result.astype(out.dtype)
    for copy in range(copies):
        out[copy * NF : (copy + 1) * NF, :] = result


def roundtrip(place, inverse, forward, onset, blocks, summed, copies, dtype):
    rows = blocks.shape[0]
    whole = lambda i, place: (0, 0)
    part = lambda i, place: (place[0], 0, 0)
    return pl.pallas_call(
        functools.partial(roundtrip_kernel, summed, copies),
        out_shape=jax.ShapeDtypeStruct((copies * NF, LANES), dtype),
        grid_spec=pltpu.PrefetchScalarGridSpec(
            num_scalar_prefetch=1,
            grid=(1,),
            in_specs=[
                pl.BlockSpec((1,) + inverse.shape[1:], part),
                pl.BlockSpec((1,) + forward.shape[1:], part),
                pl.BlockSpec((FP, LANES), lambda i, place: (0, place[2])),
                pl.BlockSpec((rows, LANES), whole),
            ],
            out_specs=pl.BlockSpec((copies * NF, LANES), whole),
        ),
        compiler_params=pltpu.CompilerParams(vmem_limit_bytes=VMEM_LIMIT),
        name="roundtrip",
    )(place, inverse, forward, onset, blocks)


def forward_kernel(updated, *refs):
    if updated:
        direct, update, response, out, held = refs
    else:
        direct, response, out = refs
    step = pl.program_id(0)
    if updated:

        @pl.when(step == 0)
        def _():
            held[...] = update[...].astype(F32)

    tiles = direct.shape[0]
    columns = []
    for tile in range(tiles):
        for half in range(2):
            both = []
            for part in range(2):
                value = direct[tile, part, step, :, half * LANES : (half + 1) * LANES]
                if updated:
                    start = tile * NF + (half * 2 + part) * 4
                    value = value + held[pl.ds(start + step, FP, stride=16), :]
                both.append(value)
            columns.append(jnp.concatenate(both, axis=0).astype(BF16))
    stacked = jnp.concatenate(columns, axis=1)
    dims = (((1,), (1,)), ((), ()))
    first = lax.dot_general(stacked, response[0, 0], dims, preferred_element_type=F32)
    second = lax.dot_general(stacked, response[1, 0], dims, preferred_element_type=F32)
    parts = (first[:FP] - second[FP:], first[FP:] + second[:FP])
    for half in range(2):
        for part in range(2):
            start = (half * 2 + part) * 4
            out[pl.ds(start + step, FP, stride=16), :] = parts[part][:, half * LANES : (half + 1) * LANES]


def forward_product(direct, update, response):
    bins = response.shape[1]
    updated = update is not None
    in_specs = [pl.BlockSpec(direct.shape, lambda j: (0, 0, 0, 0, 0))]
    args = [direct]
    scratch = []
    if updated:
        in_specs.append(pl.BlockSpec(update.shape, lambda j: (0, 0)))
        args.append(update)
        scratch.append(pltpu.VMEM(update.shape, F32))
    in_specs.append(pl.BlockSpec((2, 1) + response.shape[2:], lambda j: (0, j, 0, 0)))
    return pl.pallas_call(
        functools.partial(forward_kernel, updated),
        out_shape=jax.ShapeDtypeStruct((NF, LANES), F32),
        grid=(bins,),
        in_specs=in_specs,
        out_specs=pl.BlockSpec((NF, LANES), lambda j: (0, 0)),
        scratch_shapes=scratch,
        compiler_params=pltpu.CompilerParams(vmem_limit_bytes=VMEM_LIMIT),
        name="forward_product",
    )(*args, response)


def adjoint_kernel(blocks, response, out, minus, held):
    step = pl.program_id(0)
    rows = []
    for part in range(2):
        halves = []
        for half in range(2):
            start = (half * 2 + part) * 4
            halves.append(blocks[pl.ds(start + step, FP, stride=16), :])
        rows.append(jnp.concatenate(halves, axis=1))
        minus[part, 0] = rows[-1]
    stacked = jnp.concatenate(rows, axis=0).astype(BF16)
    first = jnp.dot(stacked, response[0, 0], preferred_element_type=F32)
    second = jnp.dot(stacked, response[1, 0], preferred_element_type=F32)
    parts = (first[:FP] + second[FP:], first[FP:] - second[:FP])
    tiles = response.shape[3] // (2 * LANES)
    for tile in range(tiles):
        for half in range(2):
            lane = (tile * 2 + half) * LANES
            for part in range(2):
                start = tile * NF + (half * 2 + part) * 4
                held[pl.ds(start + step, FP, stride=16), :] = parts[part][:, lane : lane + LANES]

    @pl.when(step == pl.num_programs(0) - 1)
    def _():
        out[...] = held[...].astype(out.dtype)


def adjoint_product(blocks, response):
    bins, receivers, sources = response.shape[1:]
    rows = NF * sources // (2 * LANES)
    return pl.pallas_call(
        adjoint_kernel,
        out_shape=(
            jax.ShapeDtypeStruct((rows, LANES), BF16),
            jax.ShapeDtypeStruct((2, bins, FP, receivers), F32),
        ),
        grid=(bins,),
        in_specs=[
            pl.BlockSpec((NF, LANES), lambda j: (0, 0)),
            pl.BlockSpec((2, 1) + response.shape[2:], lambda j: (0, j, 0, 0)),
        ],
        out_specs=(
            pl.BlockSpec((rows, LANES), lambda j: (0, 0)),
            pl.BlockSpec((2, 1, FP, receivers), lambda j: (0, j, 0, 0)),
        ),
        scratch_shapes=[pltpu.VMEM((rows, LANES), F32)],
        compiler_params=pltpu.CompilerParams(vmem_limit_bytes=VMEM_LIMIT),
        name="adjoint_product",
    )(blocks, response)


def finish_kernel(direct, blocks, out):
    for bin_ in range(direct.shape[1]):
        for part in range(2):
            for half in range(2):
                lanes = slice(half * LANES, (half + 1) * LANES)
                value = blocks[pl.ds((half * 2 + part) * 4 + bin_, FP, stride=16), :]
                out[part, bin_, :, lanes] = direct[part, bin_, :, lanes] + value


def finish(direct, blocks):
    return pl.pallas_call(
        finish_kernel,
        out_shape=jax.ShapeDtypeStruct(direct.shape, F32),
        name="finish",
    )(direct, blocks)


def exchange(blocks, axes, count):
    shaped = blocks.reshape(count, blocks.shape[0] // count, LANES)
    return lax.all_to_all(shaped, axes, 0, 0, tiled=True).reshape(blocks.shape)


def on_device(response, direct, onset):
    groups = lax.axis_size("freq")
    tiles = lax.axis_size("tile")
    everyone = ("tile", "freq")
    own = lax.axis_index("freq")
    place = jnp.stack([own % 2, own // 4, own // 2 % 2]).astype(jnp.int32)
    inverse, forward = (jnp.asarray(table) for table in tables())
    trip = functools.partial(roundtrip, place, inverse, forward, onset)
    gathered = lax.all_gather(direct, "tile", axis=0)
    update = None
    for step in range(ITERS):
        upgoing = forward_product(gathered, update, response)
        blocks = trip(exchange(upgoing, "freq", groups), False, 1, F32)
        blocks = exchange(blocks, "freq", groups)
        partial, minus = adjoint_product(blocks, response)
        partial = exchange(partial, everyone, groups * tiles)
        if step + 1 < ITERS:
            update = exchange(trip(partial, True, tiles, BF16), everyone, groups * tiles)
        else:
            plus = finish(direct, exchange(trip(partial, True, 1, F32), "freq", groups))
    return (minus, plus)


def solution(mesh):
    return jax.shard_map(
        on_device,
        mesh=mesh,
        in_specs=(P(None, "freq", "tile", None), P(None, "freq", None, "tile"), P(None, "tile")),
        out_specs=(P(None, "freq", None, "tile"), P(None, "freq", None, "tile")),
        check_vma=False,
    )
```

```python
import functools
import math

import jax
import jax.numpy as jnp
import numpy as np
from jax import lax
from jax.experimental import pallas as pl
from jax.experimental.pallas import tpu as pltpu
from jax.sharding import PartitionSpec as P

NT = 512
ITERS = 2
FIRST_BIN = 16
NF = 128
FP = 8
LAGS = 224
LANES = 128
BF16 = jnp.bfloat16
F32 = jnp.float32
VMEM_LIMIT = 24 * 1024 * 1024


def split(table):
    high = table.astype(np.float32).astype(jnp.bfloat16)
    low = (table - high.astype(np.float64)).astype(np.float32).astype(jnp.bfloat16)
    return high, low


def tables():
    bins = FIRST_BIN + np.arange(NF)
    lags = np.arange(LAGS)
    angle = 2.0 * math.pi / NT * ((lags[:, None] * bins[None, :]) % NT)
    weight = np.where(lags == 0, 2.0 / NT, 4.0 / NT)
    inverse, spread, forward = [], [], []
    for table in (np.cos(angle), np.sin(angle)):
        high, low = split(table)
        inverse.append(np.concatenate([high, high, low], axis=1))
        wide = np.pad(table.reshape(LAGS, NF // 4, 4), ((0, 0), (0, 0), (0, 4))).reshape(LAGS, 2 * NF)
        high, low = split(wide)
        spread.append(np.concatenate([high, high, low], axis=1))
        high, low = split((table * weight[:, None]).T)
        forward.append(np.concatenate([high, high, low], axis=1))
    return np.stack(inverse), np.stack(spread), np.stack(forward)


def pieces(value):
    high = value.astype(BF16)
    low = (value - high.astype(F32)).astype(BF16)
    return jnp.concatenate([high, low, high], axis=0)


def in_vmem(array):
    return pltpu.with_memory_space_constraint(array, pltpu.VMEM)


VMEM = pl.BlockSpec(memory_space=pltpu.VMEM)
SMEM = pl.BlockSpec(memory_space=pltpu.SMEM)
PARAMS = pltpu.CompilerParams(vmem_limit_bytes=VMEM_LIMIT)


def hold_kernel(response, held, done):
    copy = pltpu.make_async_copy(response, held, done)
    copy.start()
    copy.wait()


def hold(response):
    return pl.pallas_call(
        hold_kernel,
        out_shape=pltpu.VMEM(response.shape, response.dtype),
        in_specs=[pl.BlockSpec(memory_space=pltpu.HBM)],
        out_specs=VMEM,
        scratch_shapes=[pltpu.SemaphoreType.DMA],
        compiler_params=PARAMS,
        name="hold",
    )(pltpu.with_memory_space_constraint(response, pltpu.HBM))


def prepare_kernel(direct, out):
    for bin_ in range(direct.shape[1]):
        value = jnp.concatenate([direct[0, bin_], direct[1, bin_]], axis=0).astype(BF16)
        for copy in range(out.shape[0]):
            out[copy, bin_] = value


def prepare(direct, copies):
    parts, bins, focal, positions = direct.shape
    return pl.pallas_call(
        prepare_kernel,
        out_shape=jax.ShapeDtypeStruct((copies, bins, parts * focal, positions), BF16),
        in_specs=[VMEM],
        out_specs=VMEM,
        compiler_params=PARAMS,
        name="prepare",
    )(direct)


def forward_dots(stacked, response, bin_):
    dims = (((1,), (1,)), ((), ()))
    first = lax.dot_general(stacked, response[0, bin_], dims, preferred_element_type=F32)
    second = lax.dot_general(stacked, response[1, bin_], dims, preferred_element_type=F32)
    return first[:FP] - second[FP:], first[FP:] + second[:FP]


def first_forward_kernel(place, mine, other, direct, response, out):
    even = place[3] == 0
    for bin_ in range(response.shape[1]):
        columns = []
        for pair in range(mine.shape[0]):
            here, there = mine[pair, bin_], other[pair, bin_]
            columns.append(jnp.where(even, here, there))
            columns.append(jnp.where(even, there, here))
        parts = forward_dots(jnp.concatenate(columns, axis=1), response, bin_)
        for half in range(2):
            lanes = slice(half * LANES, (half + 1) * LANES)
            for part in range(2):
                start = (half * 2 + part) * 8 + bin_
                out[pl.ds(start, FP, stride=32), :] = parts[part][:, lanes]
                out[pl.ds(start + 4, FP, stride=32), :] = direct[part, bin_, :, lanes]


def first_forward(place, mine, other, direct, response):
    return pl.pallas_call(
        first_forward_kernel,
        out_shape=jax.ShapeDtypeStruct((2 * NF, LANES), F32),
        in_specs=[SMEM, VMEM, VMEM, VMEM, VMEM],
        out_specs=VMEM,
        compiler_params=PARAMS,
        name="first_forward",
    )(place, mine, other, direct, in_vmem(response))


def forward_kernel(update, response, out, held):
    held[...] = update[...].astype(F32)
    tiles = update.shape[0] // NF
    for bin_ in range(response.shape[1]):
        columns = []
        for tile in range(tiles):
            for half in range(2):
                both = []
                for part in range(2):
                    start = tile * NF + (half * 2 + part) * 4 + bin_
                    both.append(held[pl.ds(start, FP, stride=16), :])
                columns.append(jnp.concatenate(both, axis=0).astype(BF16))
        parts = forward_dots(jnp.concatenate(columns, axis=1), response, bin_)
        for half in range(2):
            for part in range(2):
                start = (half * 2 + part) * 4 + bin_
                out[pl.ds(start, FP, stride=16), :] = parts[part][:, half * LANES : (half + 1) * LANES]


def forward_product(update, response):
    return pl.pallas_call(
        forward_kernel,
        out_shape=jax.ShapeDtypeStruct((NF, LANES), F32),
        in_specs=[VMEM, VMEM],
        out_specs=VMEM,
        scratch_shapes=[pltpu.VMEM(update.shape, F32)],
        compiler_params=PARAMS,
        name="forward_product",
    )(update, in_vmem(response))


def adjoint_kernel(blocks, response, out, minus, held):
    tiles = response.shape[3] // (2 * LANES)
    for bin_ in range(response.shape[1]):
        rows = []
        for part in range(2):
            halves = []
            for half in range(2):
                start = (half * 2 + part) * 4 + bin_
                halves.append(blocks[pl.ds(start, FP, stride=16), :])
            rows.append(jnp.concatenate(halves, axis=1))
            minus[part, bin_] = rows[-1]
        stacked = jnp.concatenate(rows, axis=0).astype(BF16)
        first = jnp.dot(stacked, response[0, bin_], preferred_element_type=F32)
        second = jnp.dot(stacked, response[1, bin_], preferred_element_type=F32)
        parts = (first[:FP] + second[FP:], first[FP:] - second[:FP])
        for tile in range(tiles):
            for half in range(2):
                lane = (tile * 2 + half) * LANES
                for part in range(2):
                    start = tile * NF + (half * 2 + part) * 4 + bin_
                    held[pl.ds(start, FP, stride=16), :] = parts[part][:, lane : lane + LANES]
    out[...] = held[...].astype(out.dtype)


def adjoint_product(blocks, response):
    bins, receivers, sources = response.shape[1:]
    rows = NF * sources // (2 * LANES)
    return pl.pallas_call(
        adjoint_kernel,
        out_shape=(
            jax.ShapeDtypeStruct((rows, LANES), BF16),
            jax.ShapeDtypeStruct((2, bins, FP, receivers), F32),
        ),
        in_specs=[VMEM, VMEM],
        out_specs=(VMEM, VMEM),
        scratch_shapes=[pltpu.VMEM((rows, LANES), F32)],
        compiler_params=PARAMS,
        name="adjoint_product",
    )(blocks, in_vmem(response))


def lag_domain(spectrum, place, inverse, forward, onset):
    signal = jnp.dot(inverse[0], pieces(spectrum), preferred_element_type=F32)
    focal = lax.broadcasted_iota(jnp.int32, onset.shape, 0)
    limit = jnp.sum(jnp.where(focal == place[1], onset[...], 0), axis=0, keepdims=True)
    lag = lax.broadcasted_iota(jnp.int32, signal.shape, 0)
    signal = jnp.where(lag < limit, signal, 0.0)
    return jnp.dot(forward[0], pieces(signal), preferred_element_type=F32)


def minus_kernel(place, inverse, forward, onset, blocks, out):
    out[...] = lag_domain(blocks[...], place, inverse, forward, onset)


def plus_kernel(place, inverse, forward, onset, blocks, direct, out, held):
    spectrum = blocks[:NF, :].astype(F32)
    for tile in range(1, blocks.shape[0] // NF):
        spectrum += blocks[tile * NF : (tile + 1) * NF, :].astype(F32)
    held[...] = lag_domain(spectrum, place, inverse, forward, onset)
    senders = NF // 4
    for bin_ in range(4):
        held[pl.ds(bin_, senders, stride=4), :] += direct[pl.ds(4 + bin_, senders, stride=8), :]
    result = held[...].astype(out.dtype)
    for copy in range(out.shape[0] // NF):
        out[copy * NF : (copy + 1) * NF, :] = result


def roundtrip(kernel, place, tables, onset, operands, copies, dtype, scratch=()):
    whole = lambda i, place: (0, 0)
    part = lambda i, place: (place[0], 0, 0)
    in_specs = [pl.BlockSpec((1,) + table.shape[1:], part) for table in tables]
    in_specs.append(pl.BlockSpec((FP, LANES), lambda i, place: (0, place[2])))
    in_specs += [pl.BlockSpec(operand.shape, whole) for operand in operands]
    return pl.pallas_call(
        kernel,
        out_shape=jax.ShapeDtypeStruct((copies * NF, LANES), dtype),
        grid_spec=pltpu.PrefetchScalarGridSpec(
            num_scalar_prefetch=1,
            grid=(1,),
            in_specs=in_specs,
            out_specs=pl.BlockSpec((copies * NF, LANES), whole),
            scratch_shapes=list(scratch),
        ),
        compiler_params=PARAMS,
        name="roundtrip",
    )(place, *tables, onset, *operands)


def finish_kernel(blocks, out):
    for bin_ in range(out.shape[1]):
        for part in range(2):
            for half in range(2):
                value = blocks[pl.ds((half * 2 + part) * 4 + bin_, FP, stride=16), :]
                out[part, bin_, :, half * LANES : (half + 1) * LANES] = value


def finish(blocks, shape):
    return pl.pallas_call(
        finish_kernel,
        out_shape=jax.ShapeDtypeStruct(shape, F32),
        in_specs=[VMEM],
        out_specs=VMEM,
        compiler_params=PARAMS,
        name="finish",
    )(blocks)


def exchange(blocks, axes, count):
    shaped = blocks.reshape(count, blocks.shape[0] // count, LANES)
    return lax.all_to_all(shaped, axes, 0, 0, tiled=True).reshape(blocks.shape)


def on_device(response, direct, onset):
    groups = lax.axis_size("freq")
    tiles = lax.axis_size("tile")
    everyone = ("tile", "freq")
    own = lax.axis_index("freq")
    place = jnp.stack([own & 1, own >> 2, (own >> 1) & 1, lax.axis_index("tile") & 1]).astype(jnp.int32)
    inverse, spread, forward = (jnp.asarray(table) for table in tables())
    held = hold(response)
    pairs = tiles // 2
    chips = [[core + 2 * pair for pair in range(pairs)] for core in range(2)]
    mine = lax.all_to_all(prepare(direct, pairs), "tile", 0, 0, axis_index_groups=chips, tiled=True)
    other = lax.ppermute(mine, "tile", [(tile, tile ^ 1) for tile in range(tiles)])
    update, owned = None, None
    for step in range(ITERS):
        if step == 0:
            owned = exchange(first_forward(place, mine, other, direct, held), "freq", groups)
            blocks = roundtrip(minus_kernel, place, (spread, forward), onset, (owned,), 1, F32)
        else:
            upgoing = exchange(forward_product(update, held), "freq", groups)
            blocks = roundtrip(minus_kernel, place, (inverse, forward), onset, (upgoing,), 1, F32)
        partial, minus = adjoint_product(exchange(blocks, "freq", groups), held)
        partial = exchange(partial, everyone, groups * tiles)
        last = step + 1 == ITERS
        copies, dtype = (1, F32) if last else (tiles, BF16)
        scratch = (pltpu.VMEM((NF, LANES), F32),)
        plus = roundtrip(plus_kernel, place, (inverse, forward), onset, (partial, owned), copies, dtype, scratch)
        if last:
            plus = finish(exchange(plus, "freq", groups), direct.shape)
        else:
            update = exchange(plus, everyone, groups * tiles)
    return (minus, plus)


def solution(mesh):
    return jax.shard_map(
        on_device,
        mesh=mesh,
        in_specs=(P(None, "freq", "tile", None), P(None, "freq", None, "tile"), P(None, "tile")),
        out_specs=(P(None, "freq", None, "tile"), P(None, "freq", None, "tile")),
        check_vma=False,
    )
```

```python
import functools
import math

import jax
import jax.numpy as jnp
import numpy as np
from jax import lax
from jax.experimental import pallas as pl
from jax.experimental.pallas import tpu as pltpu
from jax.sharding import PartitionSpec as P

NT = 512
ITERS = 2
FIRST_BIN = 16
NF = 128
FP = 8
LAGS = 224
LANES = 128
BF16 = jnp.bfloat16
F32 = jnp.float32
VMEM_LIMIT = 24 * 1024 * 1024

SHARED = 64
PIECES = 16
OWNERS = 32


def split(table):
    high = table.astype(np.float32).astype(jnp.bfloat16)
    low = (table - high.astype(np.float64)).astype(np.float32).astype(jnp.bfloat16)
    return high, low


def tables():
    bins = FIRST_BIN + np.arange(NF)
    lags = np.arange(LAGS)
    angle = 2.0 * math.pi / NT * ((lags[:, None] * bins[None, :]) % NT)
    weight = np.where(lags == 0, 2.0 / NT, 4.0 / NT)
    rounded, inverse, forward, own = [], [], [], []
    devices = np.arange(OWNERS)
    pair = np.stack([devices, devices ^ (OWNERS // 2)], axis=1)
    for part, table in enumerate((np.cos(angle), np.sin(angle))):
        high, low = split(table)
        rounded.append(np.concatenate([high, low], axis=1))
        inverse.append(np.concatenate([high, high, low], axis=1))
        high, low = split((table * weight[:, None]).T)
        forward.append(np.concatenate([high, high, low], axis=1))
        high, low = (piece.reshape(OWNERS, 4, LAGS)[pair].reshape(OWNERS, 8, LAGS) for piece in (high, low))
        rows = np.concatenate(
            [np.concatenate([high, high], axis=2), np.concatenate([low, np.zeros_like(low)], axis=2)], axis=1
        )
        own.append(rows[part * OWNERS // 2 : (part + 1) * OWNERS // 2])
    return np.stack(rounded), np.concatenate(own), np.stack(inverse), np.stack(forward)


def high_low(value):
    high = value.astype(BF16)
    return high, (value - high.astype(F32)).astype(BF16)


def pieces(value):
    high, low = high_low(value)
    return jnp.concatenate([high, low, high], axis=0)


def in_vmem(array):
    return pltpu.with_memory_space_constraint(array, pltpu.VMEM)


VMEM = pl.BlockSpec(memory_space=pltpu.VMEM)
SMEM = pl.BlockSpec(memory_space=pltpu.SMEM)
PARAMS = pltpu.CompilerParams(vmem_limit_bytes=VMEM_LIMIT)


def prepare_kernel(direct, out):
    for bin_ in range(direct.shape[1]):
        value = jnp.concatenate([direct[0, bin_], direct[1, bin_]], axis=0).astype(BF16)
        for copy in range(out.shape[0]):
            out[copy, bin_] = value


def prepare(direct, copies):
    parts, bins, focal, positions = direct.shape
    return pl.pallas_call(
        prepare_kernel,
        out_shape=jax.ShapeDtypeStruct((copies, bins, parts * focal, positions), BF16),
        in_specs=[VMEM],
        out_specs=VMEM,
        compiler_params=PARAMS,
        name="prepare",
    )(direct)


def forward_dots(stacked, response, bin_):
    dims = (((1,), (1,)), ((), ()))
    first = lax.dot_general(stacked, response[0, bin_], dims, preferred_element_type=F32)
    second = lax.dot_general(stacked, response[1, bin_], dims, preferred_element_type=F32)
    return first[:FP] - second[FP:], first[FP:] + second[:FP]


def share(parts, bin_, out, stride):
    for part in range(2):
        tile = jnp.concatenate([parts[part][:, :LANES], parts[part][:, LANES:]], axis=0).astype(BF16)
        for owner in range(part * OWNERS // 2, (part + 1) * OWNERS // 2):
            start = owner * stride + bin_ * 16
            out[start : start + 16, :] = tile


def first_forward_kernel(place, mine, other, direct, response, out, kept, held, done):
    bins = response.shape[1]
    copies = [
        [pltpu.make_async_copy(response.at[part, bin_], kept.at[part, bin_], done.at[part, bin_]) for part in range(2)]
        for bin_ in range(bins)
    ]
    for both in copies:
        for copy in both:
            copy.start()
    stride = SHARED + PIECES
    held[...] = jnp.zeros_like(held)
    for bin_ in range(bins):
        for half in range(2):
            for part in range(2):
                value = direct[part, bin_, :, half * LANES : (half + 1) * LANES]
                start = (half * 2 + part) * PIECES + bin_
                for row, piece in enumerate(high_low(value)):
                    held[pl.ds(start + 4 * row, FP, stride=4 * PIECES), :] = piece.astype(F32)
    for owner in range(OWNERS):
        start = owner * stride + SHARED
        out[start : start + PIECES, :] = held[owner * PIECES : (owner + 1) * PIECES, :].astype(BF16)
    even = place[3] == 0
    for bin_ in range(bins):
        columns = []
        for pair in range(mine.shape[0]):
            here, there = mine[pair, bin_], other[pair, bin_]
            columns.append(jnp.where(even, here, there))
            columns.append(jnp.where(even, there, here))
        for copy in copies[bin_]:
            copy.wait()
        share(forward_dots(jnp.concatenate(columns, axis=1), kept, bin_), bin_, out, stride)


def first_forward(place, mine, other, direct, response):
    return pl.pallas_call(
        first_forward_kernel,
        out_shape=(
            jax.ShapeDtypeStruct((OWNERS * (SHARED + PIECES), LANES), BF16),
            pltpu.VMEM(response.shape, response.dtype),
        ),
        in_specs=[SMEM, VMEM, VMEM, VMEM, pl.BlockSpec(memory_space=pltpu.HBM)],
        out_specs=(VMEM, VMEM),
        scratch_shapes=[
            pltpu.VMEM((OWNERS * PIECES, LANES), F32),
            pltpu.SemaphoreType.DMA(response.shape[:2]),
        ],
        compiler_params=PARAMS,
        name="first_forward",
    )(place, mine, other, direct, pltpu.with_memory_space_constraint(response, pltpu.HBM))


def forward_kernel(update, response, out, held):
    held[...] = update[...].astype(F32)
    tiles = update.shape[0] // NF
    for bin_ in range(response.shape[1]):
        columns = []
        for tile in range(tiles):
            for half in range(2):
                both = []
                for part in range(2):
                    start = tile * NF + (half * 2 + part) * 4 + bin_
                    both.append(held[pl.ds(start, FP, stride=16), :])
                columns.append(jnp.concatenate(both, axis=0).astype(BF16))
        share(forward_dots(jnp.concatenate(columns, axis=1), response, bin_), bin_, out, SHARED)


def forward_product(update, response):
    return pl.pallas_call(
        forward_kernel,
        out_shape=jax.ShapeDtypeStruct((OWNERS * SHARED, LANES), BF16),
        in_specs=[VMEM, VMEM],
        out_specs=VMEM,
        scratch_shapes=[pltpu.VMEM(update.shape, F32)],
        compiler_params=PARAMS,
        name="forward_product",
    )(update, in_vmem(response))


def minus_kernel(stride, place, rounded, own, onset, blocks, mine, other, *refs):
    *owned, spectra = refs
    for owner in range(OWNERS):
        start = owner * stride
        spectra[owner * SHARED : (owner + 1) * SHARED, :] = blocks[start : start + SHARED, :].astype(F32)
    inverse = rounded[place[4] // (OWNERS // 2)]
    forward = own[place[4]]
    wide = 2
    for half in range(2):
        lanes = slice(half * LANES, (half + 1) * LANES)
        for focal in range(0, FP, wide):
            first = half * FP + focal
            spectrum = jnp.concatenate(
                [spectra[pl.ds(first + i, NF, stride=16), :].astype(BF16) for i in range(wide)], axis=1
            )
            spectrum = jnp.concatenate([spectrum, spectrum], axis=0)
            signal = jnp.dot(inverse, spectrum, preferred_element_type=F32)
            limit = jnp.concatenate([onset[focal + i : focal + i + 1, lanes] for i in range(wide)], axis=1)
            lag = lax.broadcasted_iota(jnp.int32, signal.shape, 0)
            signal = jnp.where(lag < limit, signal, 0.0)
            signal = jnp.concatenate(high_low(signal), axis=0)
            result = jnp.dot(forward, signal, preferred_element_type=F32)
            result = result[:8] + result[8:]
            for i in range(wide):
                block = result[:, i * LANES : (i + 1) * LANES]
                mine[pl.ds(first + i, 4, stride=16), :] = block[:4]
                other[pl.ds(first + i, 4, stride=16), :] = block[4:]
    if owned:
        (owned,) = owned
        for owner in range(OWNERS):
            start = owner * stride + SHARED
            spectra[owner * PIECES : (owner + 1) * PIECES, :] = blocks[start : start + PIECES, :].astype(F32)
        for bin_ in range(4):
            high, low = (spectra[pl.ds(bin_ + 4 * i, OWNERS, stride=PIECES), :] for i in range(2))
            owned[pl.ds(bin_, OWNERS, stride=4), :] = high + low


def minus_roundtrip(place, rounded, own, onset, blocks, carried):
    stride = SHARED + PIECES if carried else SHARED
    out_shape = [jax.ShapeDtypeStruct((SHARED, LANES), F32)] * 2
    if carried:
        out_shape.append(jax.ShapeDtypeStruct((NF, LANES), F32))
    return pl.pallas_call(
        functools.partial(minus_kernel, stride),
        out_shape=out_shape,
        in_specs=[SMEM] + [VMEM] * 4,
        out_specs=[VMEM] * len(out_shape),
        scratch_shapes=[pltpu.VMEM((OWNERS * SHARED, LANES), F32)],
        compiler_params=PARAMS,
        name="minus_roundtrip",
    )(place, rounded, own, onset, blocks)


def adjoint_kernel(place, mine, other, response, out, minus, held):
    lower = place[4] < OWNERS // 2
    tiles = response.shape[3] // (2 * LANES)
    for bin_ in range(response.shape[1]):
        here, there = (
            jnp.concatenate([part[start : start + FP, :] for start in (bin_ * 16, bin_ * 16 + FP)], axis=1)
            for part in (mine, other)
        )
        both = jnp.where(lower, here, there), jnp.where(lower, there, here)
        for part in range(2):
            minus[part, bin_] = both[part]
        stacked = jnp.concatenate(both, axis=0).astype(BF16)
        first = jnp.dot(stacked, response[0, bin_], preferred_element_type=F32)
        second = jnp.dot(stacked, response[1, bin_], preferred_element_type=F32)
        parts = (first[:FP] + second[FP:], first[FP:] - second[:FP])
        for tile in range(tiles):
            for half in range(2):
                lane = (tile * 2 + half) * LANES
                for part in range(2):
                    start = tile * NF + (half * 2 + part) * 4 + bin_
                    held[pl.ds(start, FP, stride=16), :] = parts[part][:, lane : lane + LANES]
    out[...] = held[...].astype(out.dtype)


def adjoint_product(place, mine, other, response):
    bins, receivers, sources = response.shape[1:]
    rows = NF * sources // (2 * LANES)
    return pl.pallas_call(
        adjoint_kernel,
        out_shape=(
            jax.ShapeDtypeStruct((rows, LANES), BF16),
            jax.ShapeDtypeStruct((2, bins, FP, receivers), F32),
        ),
        in_specs=[SMEM] + [VMEM] * 3,
        out_specs=(VMEM, VMEM),
        scratch_shapes=[pltpu.VMEM((rows, LANES), F32)],
        compiler_params=PARAMS,
        name="adjoint_product",
    )(place, mine, other, in_vmem(response))


def plus_kernel(place, inverse, forward, onset, blocks, direct, out):
    spectrum = blocks[:NF, :].astype(F32)
    for tile in range(1, blocks.shape[0] // NF):
        spectrum += blocks[tile * NF : (tile + 1) * NF, :].astype(F32)
    signal = jnp.dot(inverse[place[0]], pieces(spectrum), preferred_element_type=F32)
    limits = jnp.where(place[2] == 0, onset[:, :LANES], onset[:, LANES:])
    focal = lax.broadcasted_iota(jnp.int32, limits.shape, 0)
    limit = jnp.sum(jnp.where(focal == place[1], limits, 0), axis=0, keepdims=True)
    lag = lax.broadcasted_iota(jnp.int32, signal.shape, 0)
    signal = jnp.where(lag < limit, signal, 0.0)
    result = jnp.dot(forward[place[0]], pieces(signal), preferred_element_type=F32)
    result = (direct[...] + result).astype(out.dtype)
    for copy in range(out.shape[0] // NF):
        out[copy * NF : (copy + 1) * NF, :] = result


def plus_roundtrip(place, inverse, forward, onset, blocks, direct, copies, dtype):
    return pl.pallas_call(
        plus_kernel,
        out_shape=jax.ShapeDtypeStruct((copies * NF, LANES), dtype),
        in_specs=[SMEM] + [VMEM] * 5,
        out_specs=VMEM,
        compiler_params=PARAMS,
        name="plus_roundtrip",
    )(place, inverse, forward, onset, blocks, direct)


def finish_kernel(blocks, out):
    for bin_ in range(out.shape[1]):
        for part in range(2):
            for half in range(2):
                value = blocks[pl.ds((half * 2 + part) * 4 + bin_, FP, stride=16), :]
                out[part, bin_, :, half * LANES : (half + 1) * LANES] = value


def finish(blocks, shape):
    return pl.pallas_call(
        finish_kernel,
        out_shape=jax.ShapeDtypeStruct(shape, F32),
        in_specs=[VMEM],
        out_specs=VMEM,
        compiler_params=PARAMS,
        name="finish",
    )(blocks)


def exchange(blocks, axes, count):
    shaped = blocks.reshape(count, blocks.shape[0] // count, LANES)
    return lax.all_to_all(shaped, axes, 0, 0, tiled=True).reshape(blocks.shape)


def on_device(response, direct, onset):
    groups = lax.axis_size("freq")
    tiles = lax.axis_size("tile")
    everyone = ("tile", "freq")
    own = lax.axis_index("freq")
    place = [own & 1, own >> 2, (own >> 1) & 1, lax.axis_index("tile") & 1, own]
    place = jnp.stack(place).astype(jnp.int32)
    rounded, own_bins, inverse, forward = (jnp.asarray(table) for table in tables())
    pairs = tiles // 2
    chips = [[core + 2 * pair for pair in range(pairs)] for core in range(2)]
    cores = [(tile, tile ^ 1) for tile in range(tiles)]
    partners = [(owner, owner ^ (OWNERS // 2)) for owner in range(OWNERS)]
    mine = lax.all_to_all(prepare(direct, pairs), "tile", 0, 0, axis_index_groups=chips, tiled=True)
    other = lax.ppermute(mine, "tile", cores)
    for step in range(ITERS):
        if step == 0:
            upgoing, held = first_forward(place, mine, other, direct, response)
        else:
            upgoing = forward_product(update, held)
        upgoing = exchange(upgoing, "freq", groups)
        mine, other, *owned = minus_roundtrip(place, rounded, own_bins, onset, upgoing, step == 0)
        if step == 0:
            (direct_columns,) = owned
        partial, minus = adjoint_product(place, mine, lax.ppermute(other, "freq", partners), held)
        partial = exchange(partial, everyone, groups * tiles)
        last = step + 1 == ITERS
        copies, dtype = (1, F32) if last else (tiles, BF16)
        plus = plus_roundtrip(place, inverse, forward, onset, partial, direct_columns, copies, dtype)
        if last:
            plus = finish(exchange(plus, "freq", groups), direct.shape)
        else:
            update = exchange(plus, everyone, groups * tiles)
    return (minus, plus)


def solution(mesh):
    return jax.shard_map(
        on_device,
        mesh=mesh,
        in_specs=(P(None, "freq", "tile", None), P(None, "freq", None, "tile"), P(None, "tile")),
        out_specs=(P(None, "freq", None, "tile"), P(None, "freq", None, "tile")),
        check_vma=False,
    )
```

```python
import functools
import math

import jax
import jax.numpy as jnp
import numpy as np
from jax import lax
from jax.experimental import pallas as pl
from jax.experimental.pallas import tpu as pltpu
from jax.sharding import PartitionSpec as P

NT = 512
ITERS = 2
FIRST_BIN = 16
NF = 128
FP = 8
LAGS = 224
LANES = 128
BF16 = jnp.bfloat16
F32 = jnp.float32
VMEM_LIMIT = 24 * 1024 * 1024

SHARED = 64
PIECES = 16
OWNERS = 32


def split(table):
    high = table.astype(np.float32).astype(jnp.bfloat16)
    low = (table - high.astype(np.float64)).astype(np.float32).astype(jnp.bfloat16)
    return high, low


def tables():
    bins = FIRST_BIN + np.arange(NF)
    lags = np.arange(LAGS)
    angle = 2.0 * math.pi / NT * ((lags[:, None] * bins[None, :]) % NT)
    weight = np.where(lags == 0, 2.0 / NT, 4.0 / NT)
    rounded, inverse, forward, own = [], [], [], []
    devices = np.arange(OWNERS)
    pair = np.stack([devices, devices ^ (OWNERS // 2)], axis=1)
    for part, table in enumerate((np.cos(angle), np.sin(angle))):
        high, low = split(table)
        rounded.append(np.concatenate([high, low], axis=1))
        inverse.append(np.concatenate([high, high, low], axis=1))
        high, low = split((table * weight[:, None]).T)
        forward.append(np.concatenate([high, high, low], axis=1))
        high, low = (piece.reshape(OWNERS, 4, LAGS)[pair].reshape(OWNERS, 8, LAGS) for piece in (high, low))
        rows = np.concatenate(
            [np.concatenate([high, high], axis=2), np.concatenate([low, np.zeros_like(low)], axis=2)], axis=1
        )
        own.append(rows[part * OWNERS // 2 : (part + 1) * OWNERS // 2])
    return np.stack(rounded), np.concatenate(own), np.stack(inverse), np.stack(forward)


def high_low(value):
    high = value.astype(BF16)
    return high, (value - high.astype(F32)).astype(BF16)


def pieces(value):
    high, low = high_low(value)
    return jnp.concatenate([high, low, high], axis=0)


def in_vmem(array):
    return pltpu.with_memory_space_constraint(array, pltpu.VMEM)


def in_hbm(array):
    return pltpu.with_memory_space_constraint(array, pltpu.HBM)


VMEM = pl.BlockSpec(memory_space=pltpu.VMEM)
HBM = pl.BlockSpec(memory_space=pltpu.HBM)
PARAMS = pltpu.CompilerParams(vmem_limit_bytes=VMEM_LIMIT)


def hold_kernel(response, held, done):
    copy = pltpu.make_async_copy(response, held, done)
    copy.start()
    copy.wait()


def hold(response):
    return pl.pallas_call(
        hold_kernel,
        out_shape=pltpu.VMEM(response.shape, response.dtype),
        in_specs=[HBM],
        out_specs=VMEM,
        scratch_shapes=[pltpu.SemaphoreType.DMA],
        compiler_params=PARAMS,
        cost_estimate=pl.CostEstimate(flops=0, bytes_accessed=4 * response.size, transcendentals=0),
        name="hold",
    )(in_hbm(response))


def prepare_kernel(mine, other, out):
    even = lax.axis_index("core") == 0
    for bin_ in range(mine.shape[1]):
        here, there = (jnp.concatenate([direct[0, bin_], direct[1, bin_]], axis=0) for direct in (mine, other))
        out[0, bin_] = jnp.where(even, here, there).astype(BF16)
        out[1, bin_] = jnp.where(even, there, here).astype(BF16)


def prepare(mine, other):
    parts, bins, focal, positions = mine.shape
    return pl.pallas_call(
        prepare_kernel,
        out_shape=jax.ShapeDtypeStruct((2, bins, parts * focal, positions), BF16),
        in_specs=[VMEM, VMEM],
        out_specs=VMEM,
        compiler_params=PARAMS,
        name="prepare",
    )(mine, other)


def forward_dots(stacked, response, bin_):
    dims = (((1,), (1,)), ((), ()))
    first = lax.dot_general(stacked, response[0, bin_], dims, preferred_element_type=F32)
    second = lax.dot_general(stacked, response[1, bin_], dims, preferred_element_type=F32)
    return first[:FP] - second[FP:], first[FP:] + second[:FP]


def share(parts, bin_, out, stride):
    for part in range(2):
        tile = jnp.concatenate([parts[part][:, :LANES], parts[part][:, LANES:]], axis=0).astype(BF16)
        for owner in range(part * OWNERS // 2, (part + 1) * OWNERS // 2):
            start = owner * stride + bin_ * 16
            out[start : start + 16, :] = tile


def spread_direct(direct, held, out, stride):
    held[...] = jnp.zeros_like(held)
    for bin_ in range(direct.shape[1]):
        for half in range(2):
            for part in range(2):
                value = direct[part, bin_, :, half * LANES : (half + 1) * LANES]
                start = (half * 2 + part) * PIECES + bin_
                for row, piece in enumerate(high_low(value)):
                    held[pl.ds(start + 4 * row, FP, stride=4 * PIECES), :] = piece.astype(F32)
    for owner in range(OWNERS):
        start = owner * stride + SHARED
        out[start : start + PIECES, :] = held[owner * PIECES : (owner + 1) * PIECES, :].astype(BF16)


def first_forward_kernel(*refs):
    *gathered, direct, response, out, near, stacked, held, near_done = refs
    fetch = pltpu.make_async_copy(direct, near, near_done)
    fetch.start()
    stride = SHARED + PIECES
    pairs = len(gathered)
    positions = gathered[0].shape[3]
    for shift in range(pairs):
        pair = (lax.axis_index("pair") - shift + pairs) & (pairs - 1)
        for core in range(2):
            start = pl.multiple_of((2 * pair + core) * positions, positions)
            for bin_ in range(response.shape[1]):
                stacked[bin_, :, pl.ds(start, positions)] = gathered[shift][core, bin_]
    for bin_ in range(response.shape[1]):
        share(forward_dots(stacked[bin_], response, bin_), bin_, out, stride)
    fetch.wait()
    spread_direct(near, held, out, stride)


def first_forward(gathered, direct, response):
    bins, sources = response.shape[1], response.shape[3]
    return pl.pallas_call(
        first_forward_kernel,
        out_shape=jax.ShapeDtypeStruct((OWNERS * (SHARED + PIECES), LANES), BF16),
        in_specs=[VMEM] * len(gathered) + [HBM, VMEM],
        out_specs=VMEM,
        scratch_shapes=[
            pltpu.VMEM(direct.shape, F32),
            pltpu.VMEM((bins, 2 * FP, sources), BF16),
            pltpu.VMEM((OWNERS * PIECES, LANES), F32),
            pltpu.SemaphoreType.DMA,
        ],
        compiler_params=PARAMS,
        name="first_forward",
    )(*gathered, in_hbm(direct), in_vmem(response))


def forward_kernel(mine, other, response, out, held):
    own_core = lax.axis_index("core")
    pairs = mine.shape[0] // NF
    for pair in range(pairs):
        for source, core in ((mine, own_core), (other, 1 - own_core)):
            start = pl.multiple_of((2 * pair + core) * NF, NF)
            held[pl.ds(start, NF), :] = source[pair * NF : (pair + 1) * NF, :].astype(F32)
    for bin_ in range(response.shape[1]):
        columns = []
        for tile in range(2 * pairs):
            for half in range(2):
                both = []
                for part in range(2):
                    start = tile * NF + (half * 2 + part) * 4 + bin_
                    both.append(held[pl.ds(start, FP, stride=16), :])
                columns.append(jnp.concatenate(both, axis=0).astype(BF16))
        share(forward_dots(jnp.concatenate(columns, axis=1), response, bin_), bin_, out, SHARED)


def forward_product(mine, other, response):
    return pl.pallas_call(
        forward_kernel,
        out_shape=jax.ShapeDtypeStruct((OWNERS * SHARED, LANES), BF16),
        in_specs=[VMEM] * 3,
        out_specs=VMEM,
        scratch_shapes=[pltpu.VMEM((2 * mine.shape[0], LANES), F32)],
        compiler_params=PARAMS,
        name="forward_product",
    )(mine, other, in_vmem(response))


def minus_kernel(stride, rounded, own, onset, blocks, mine, other, *refs):
    *owned, spectra = refs
    for owner in range(OWNERS):
        start = owner * stride
        spectra[owner * SHARED : (owner + 1) * SHARED, :] = blocks[start : start + SHARED, :].astype(F32)
    device = lax.axis_index("freq")
    inverse = rounded[device >> 4]
    forward = own[device]
    wide = 2
    for half in range(2):
        lanes = slice(half * LANES, (half + 1) * LANES)
        for focal in range(0, FP, wide):
            first = half * FP + focal
            spectrum = jnp.concatenate(
                [spectra[pl.ds(first + i, NF, stride=16), :].astype(BF16) for i in range(wide)], axis=1
            )
            spectrum = jnp.concatenate([spectrum, spectrum], axis=0)
            signal = jnp.dot(inverse, spectrum, preferred_element_type=F32)
            limit = jnp.concatenate([onset[focal + i : focal + i + 1, lanes] for i in range(wide)], axis=1)
            lag = lax.broadcasted_iota(jnp.int32, signal.shape, 0)
            signal = jnp.where(lag < limit, signal, 0.0)
            signal = jnp.concatenate(high_low(signal), axis=0)
            result = jnp.dot(forward, signal, preferred_element_type=F32)
            result = result[:8] + result[8:]
            for i in range(wide):
                block = result[:, i * LANES : (i + 1) * LANES]
                mine[pl.ds(first + i, 4, stride=16), :] = block[:4]
                other[pl.ds(first + i, 4, stride=16), :] = block[4:]
    if owned:
        (owned,) = owned
        for owner in range(OWNERS):
            start = owner * stride + SHARED
            spectra[owner * PIECES : (owner + 1) * PIECES, :] = blocks[start : start + PIECES, :].astype(F32)
        for bin_ in range(4):
            high, low = (spectra[pl.ds(bin_ + 4 * i, OWNERS, stride=PIECES), :] for i in range(2))
            owned[pl.ds(bin_, OWNERS, stride=4), :] = high + low


def minus_roundtrip(rounded, own, onset, blocks, carried):
    stride = SHARED + PIECES if carried else SHARED
    out_shape = [jax.ShapeDtypeStruct((SHARED, LANES), F32)] * 2
    if carried:
        out_shape.append(jax.ShapeDtypeStruct((NF, LANES), F32))
    return pl.pallas_call(
        functools.partial(minus_kernel, stride),
        out_shape=out_shape,
        in_specs=[VMEM] * 4,
        out_specs=[VMEM] * len(out_shape),
        scratch_shapes=[pltpu.VMEM((OWNERS * SHARED, LANES), F32)],
        compiler_params=PARAMS,
        name="minus_roundtrip",
    )(rounded, own, onset, blocks)


def adjoint_kernel(mine, other, response, out, minus, held):
    lower = lax.axis_index("freq") < OWNERS // 2
    tiles = response.shape[3] // (2 * LANES)
    for bin_ in range(response.shape[1]):
        here, there = (
            jnp.concatenate([part[start : start + FP, :] for start in (bin_ * 16, bin_ * 16 + FP)], axis=1)
            for part in (mine, other)
        )
        both = jnp.where(lower, here, there), jnp.where(lower, there, here)
        for part in range(2):
            minus[part, bin_] = both[part]
        stacked = jnp.concatenate(both, axis=0).astype(BF16)
        first = jnp.dot(stacked, response[0, bin_], preferred_element_type=F32)
        second = jnp.dot(stacked, response[1, bin_], preferred_element_type=F32)
        parts = (first[:FP] + second[FP:], first[FP:] - second[:FP])
        for tile in range(tiles):
            for half in range(2):
                lane = (tile * 2 + half) * LANES
                for part in range(2):
                    start = tile * NF + (half * 2 + part) * 4 + bin_
                    held[pl.ds(start, FP, stride=16), :] = parts[part][:, lane : lane + LANES]
    out[...] = held[...].astype(out.dtype)


def adjoint_product(mine, other, response):
    bins, receivers, sources = response.shape[1:]
    rows = NF * sources // (2 * LANES)
    return pl.pallas_call(
        adjoint_kernel,
        out_shape=(
            jax.ShapeDtypeStruct((rows, LANES), BF16),
            jax.ShapeDtypeStruct((2, bins, FP, receivers), F32),
        ),
        in_specs=[VMEM] * 3,
        out_specs=(VMEM, VMEM),
        scratch_shapes=[pltpu.VMEM((rows, LANES), F32)],
        compiler_params=PARAMS,
        name="adjoint_product",
    )(mine, other, in_vmem(response))


def plus_kernel(inverse, forward, onset, blocks, direct, out):
    device = lax.axis_index("freq")
    part, own_half, own_focal = device & 1, (device >> 1) & 1, device >> 2
    spectrum = blocks[:NF, :].astype(F32)
    for tile in range(1, blocks.shape[0] // NF):
        spectrum += blocks[tile * NF : (tile + 1) * NF, :].astype(F32)
    signal = jnp.dot(inverse[part], pieces(spectrum), preferred_element_type=F32)
    limits = jnp.where(own_half == 0, onset[:, :LANES], onset[:, LANES:])
    focal = lax.broadcasted_iota(jnp.int32, limits.shape, 0)
    limit = jnp.sum(jnp.where(focal == own_focal, limits, 0), axis=0, keepdims=True)
    lag = lax.broadcasted_iota(jnp.int32, signal.shape, 0)
    signal = jnp.where(lag < limit, signal, 0.0)
    result = jnp.dot(forward[part], pieces(signal), preferred_element_type=F32)
    result = (direct[...] + result).astype(out.dtype)
    for copy in range(out.shape[0] // NF):
        out[copy * NF : (copy + 1) * NF, :] = result


def plus_roundtrip(inverse, forward, onset, blocks, direct, copies, dtype):
    return pl.pallas_call(
        plus_kernel,
        out_shape=jax.ShapeDtypeStruct((copies * NF, LANES), dtype),
        in_specs=[VMEM] * 5,
        out_specs=VMEM,
        compiler_params=PARAMS,
        name="plus_roundtrip",
    )(inverse, forward, onset, blocks, direct)


def finish_kernel(blocks, out):
    for bin_ in range(out.shape[1]):
        for part in range(2):
            for half in range(2):
                value = blocks[pl.ds((half * 2 + part) * 4 + bin_, FP, stride=16), :]
                out[part, bin_, :, half * LANES : (half + 1) * LANES] = value


def finish(blocks, shape):
    return pl.pallas_call(
        finish_kernel,
        out_shape=jax.ShapeDtypeStruct(shape, F32),
        in_specs=[VMEM],
        out_specs=VMEM,
        compiler_params=PARAMS,
        name="finish",
    )(blocks)


def exchange(blocks, axes, count):
    shaped = blocks.reshape(count, blocks.shape[0] // count, LANES)
    return lax.all_to_all(shaped, axes, 0, 0, tiled=True).reshape(blocks.shape)


def on_device(response, direct, onset):
    groups, pairs, cores = (lax.axis_size(axis) for axis in ("freq", "pair", "core"))
    rounded, own_bins, inverse, forward = (jnp.asarray(table) for table in tables())
    other_core = functools.partial(lax.ppermute, axis_name="core", perm=[(0, 1), (1, 0)])
    partners = [(owner, owner ^ (OWNERS // 2)) for owner in range(OWNERS)]
    chip = prepare(direct, other_core(direct))
    gathered = [chip]
    for shift in range(1, pairs):
        gathered.append(lax.ppermute(chip, "pair", [(pair, (pair + shift) % pairs) for pair in range(pairs)]))
    held = hold(response)
    for step in range(ITERS):
        if step == 0:
            upgoing = first_forward(gathered, direct, held)
        else:
            upgoing = forward_product(mine, other, held)
        upgoing = exchange(upgoing, "freq", groups)
        mine, other, *owned = minus_roundtrip(rounded, own_bins, onset, upgoing, step == 0)
        if step == 0:
            (direct_columns,) = owned
        partial, minus = adjoint_product(mine, lax.ppermute(other, "freq", partners), held)
        partial = exchange(partial, ("pair", "core", "freq"), pairs * cores * groups)
        last = step + 1 == ITERS
        copies, dtype = (1, F32) if last else (pairs, BF16)
        plus = plus_roundtrip(inverse, forward, onset, partial, direct_columns, copies, dtype)
        if last:
            plus = finish(exchange(plus, "freq", groups), direct.shape)
        else:
            mine = exchange(plus, ("pair", "freq"), pairs * groups)
            other = other_core(mine)
    return (minus, plus)


def solution(mesh):
    groups, tiles = mesh.devices.shape
    devices = mesh.devices.reshape(groups, tiles // 2, 2)
    tile = ("pair", "core")
    return jax.shard_map(
        on_device,
        mesh=jax.sharding.Mesh(devices, ("freq",) + tile),
        in_specs=(P(None, "freq", tile, None), P(None, "freq", None, tile), P(None, tile)),
        out_specs=(P(None, "freq", None, tile), P(None, "freq", None, tile)),
        check_vma=False,
    )
```

```python
import functools
import math

import jax
import jax.numpy as jnp
import numpy as np
from jax import lax
from jax.experimental import pallas as pl
from jax.experimental.pallas import tpu as pltpu
from jax.sharding import PartitionSpec as P

NT = 512
ITERS = 2
FIRST_BIN = 16
NF = 128
FP = 8
LAGS = 224
LANES = 128
BF16 = jnp.bfloat16
F32 = jnp.float32
VMEM_LIMIT = 24 * 1024 * 1024

SHARED = 64
PIECES = 16
OWNERS = 32


def split(table):
    high = table.astype(np.float32).astype(jnp.bfloat16)
    low = (table - high.astype(np.float64)).astype(np.float32).astype(jnp.bfloat16)
    return high, low


def tables():
    bins = FIRST_BIN + np.arange(NF)
    lags = np.arange(LAGS)
    angle = 2.0 * math.pi / NT * ((lags[:, None] * bins[None, :]) % NT)
    weight = np.where(lags == 0, 2.0 / NT, 4.0 / NT)
    rounded, inverse, forward, own = [], [], [], []
    devices = np.arange(OWNERS)
    pair = np.stack([devices, devices ^ (OWNERS // 2)], axis=1)
    for part, table in enumerate((np.cos(angle), np.sin(angle))):
        high, low = split(table)
        rounded.append(np.concatenate([high, low], axis=1))
        inverse.append(np.concatenate([high, high, low], axis=1))
        high, low = split((table * weight[:, None]).T)
        forward.append(np.concatenate([high, high, low], axis=1))
        high, low = (piece.reshape(OWNERS, 4, LAGS)[pair].reshape(OWNERS, 8, LAGS) for piece in (high, low))
        rows = np.concatenate(
            [np.concatenate([high, high], axis=2), np.concatenate([low, np.zeros_like(low)], axis=2)], axis=1
        )
        own.append(rows[part * OWNERS // 2 : (part + 1) * OWNERS // 2])
    return np.stack(rounded), np.concatenate(own), np.stack(inverse), np.stack(forward)


def high_low(value):
    high = value.astype(BF16)
    return high, (value - high.astype(F32)).astype(BF16)


def pieces(value):
    high, low = high_low(value)
    return jnp.concatenate([high, low, high], axis=0)


def in_vmem(array):
    return pltpu.with_memory_space_constraint(array, pltpu.VMEM)


def in_hbm(array):
    return pltpu.with_memory_space_constraint(array, pltpu.HBM)


VMEM = pl.BlockSpec(memory_space=pltpu.VMEM)
HBM = pl.BlockSpec(memory_space=pltpu.HBM)
PARAMS = pltpu.CompilerParams(vmem_limit_bytes=VMEM_LIMIT)


def hold_kernel(response, held, done):
    copy = pltpu.make_async_copy(response, held, done)
    copy.start()
    copy.wait()


def hold(response):
    return pl.pallas_call(
        hold_kernel,
        out_shape=pltpu.VMEM(response.shape, response.dtype),
        in_specs=[HBM],
        out_specs=VMEM,
        scratch_shapes=[pltpu.SemaphoreType.DMA],
        compiler_params=PARAMS,
        cost_estimate=pl.CostEstimate(flops=0, bytes_accessed=4 * response.size, transcendentals=0),
        name="hold",
    )(in_hbm(response))


def prepare_kernel(direct, out):
    for bin_ in range(direct.shape[1]):
        out[bin_] = jnp.concatenate([direct[0, bin_], direct[1, bin_]], axis=0).astype(BF16)


def prepare(direct):
    parts, bins, focal, positions = direct.shape
    return pl.pallas_call(
        prepare_kernel,
        out_shape=jax.ShapeDtypeStruct((bins, parts * focal, positions), BF16),
        in_specs=[VMEM],
        out_specs=VMEM,
        compiler_params=PARAMS,
        name="prepare",
    )(direct)


def order_kernel(*refs):
    *shifted, _, out = refs
    pairs = len(shifted)
    for shift in range(pairs):
        out[(lax.axis_index("pair") - shift + pairs) & (pairs - 1)] = shifted[shift][...]


def order(shifted, held):
    return pl.pallas_call(
        order_kernel,
        out_shape=jax.ShapeDtypeStruct((len(shifted),) + shifted[0].shape, BF16),
        in_specs=[VMEM] * (len(shifted) + 1),
        out_specs=VMEM,
        compiler_params=PARAMS,
        name="order",
    )(*shifted, in_vmem(held))


def forward_dots(stacked, response, bin_):
    dims = (((1,), (1,)), ((), ()))
    first = lax.dot_general(stacked, response[0, bin_], dims, preferred_element_type=F32)
    second = lax.dot_general(stacked, response[1, bin_], dims, preferred_element_type=F32)
    return first[:FP] - second[FP:], first[FP:] + second[:FP]


def share(parts, bin_, out, stride):
    for part in range(2):
        tile = jnp.concatenate([parts[part][:, :LANES], parts[part][:, LANES:]], axis=0).astype(BF16)
        for owner in range(part * OWNERS // 2, (part + 1) * OWNERS // 2):
            start = owner * stride + bin_ * 16
            out[start : start + 16, :] = tile


def spread_direct(direct, held, out, stride):
    held[...] = jnp.zeros_like(held)
    for bin_ in range(direct.shape[1]):
        for half in range(2):
            for part in range(2):
                value = direct[part, bin_, :, half * LANES : (half + 1) * LANES]
                start = (half * 2 + part) * PIECES + bin_
                for row, piece in enumerate(high_low(value)):
                    held[pl.ds(start + 4 * row, FP, stride=4 * PIECES), :] = piece.astype(F32)
    for owner in range(OWNERS):
        start = owner * stride + SHARED
        out[start : start + PIECES, :] = held[owner * PIECES : (owner + 1) * PIECES, :].astype(BF16)


def first_forward_kernel(mine, other, direct, response, out, near, stacked, held, near_done):
    fetch = pltpu.make_async_copy(direct, near, near_done)
    fetch.start()
    stride = SHARED + PIECES
    own_core = lax.axis_index("core")
    pairs, bins, _, positions = mine.shape
    for pair in range(pairs):
        for source, core in ((mine, own_core), (other, 1 - own_core)):
            start = pl.multiple_of((2 * pair + core) * positions, positions)
            for bin_ in range(bins):
                stacked[bin_, :, pl.ds(start, positions)] = source[pair, bin_]
    for bin_ in range(bins):
        share(forward_dots(stacked[bin_], response, bin_), bin_, out, stride)
    fetch.wait()
    spread_direct(near, held, out, stride)


def first_forward(mine, other, direct, response):
    bins, sources = response.shape[1], response.shape[3]
    return pl.pallas_call(
        first_forward_kernel,
        out_shape=jax.ShapeDtypeStruct((OWNERS * (SHARED + PIECES), LANES), BF16),
        in_specs=[VMEM, VMEM, HBM, VMEM],
        out_specs=VMEM,
        scratch_shapes=[
            pltpu.VMEM(direct.shape, F32),
            pltpu.VMEM((bins, 2 * FP, sources), BF16),
            pltpu.VMEM((OWNERS * PIECES, LANES), F32),
            pltpu.SemaphoreType.DMA,
        ],
        compiler_params=PARAMS,
        name="first_forward",
    )(mine, other, in_hbm(direct), in_vmem(response))


def forward_kernel(mine, other, response, out, held):
    own_core = lax.axis_index("core")
    pairs = mine.shape[0] // NF
    for pair in range(pairs):
        for source, core in ((mine, own_core), (other, 1 - own_core)):
            start = pl.multiple_of((2 * pair + core) * NF, NF)
            held[pl.ds(start, NF), :] = source[pair * NF : (pair + 1) * NF, :].astype(F32)
    for bin_ in range(response.shape[1]):
        columns = []
        for tile in range(2 * pairs):
            for half in range(2):
                both = []
                for part in range(2):
                    start = tile * NF + (half * 2 + part) * 4 + bin_
                    both.append(held[pl.ds(start, FP, stride=16), :])
                columns.append(jnp.concatenate(both, axis=0).astype(BF16))
        share(forward_dots(jnp.concatenate(columns, axis=1), response, bin_), bin_, out, SHARED)


def forward_product(mine, other, response):
    return pl.pallas_call(
        forward_kernel,
        out_shape=jax.ShapeDtypeStruct((OWNERS * SHARED, LANES), BF16),
        in_specs=[VMEM] * 3,
        out_specs=VMEM,
        scratch_shapes=[pltpu.VMEM((2 * mine.shape[0], LANES), F32)],
        compiler_params=PARAMS,
        name="forward_product",
    )(mine, other, in_vmem(response))


def minus_kernel(stride, rounded, own, onset, blocks, mine, other, *refs):
    *owned, spectra = refs
    for owner in range(OWNERS):
        start = owner * stride
        spectra[owner * SHARED : (owner + 1) * SHARED, :] = blocks[start : start + SHARED, :].astype(F32)
    device = lax.axis_index("freq")
    inverse = rounded[device >> 4]
    forward = own[device]
    wide = 2
    for half in range(2):
        lanes = slice(half * LANES, (half + 1) * LANES)
        for focal in range(0, FP, wide):
            first = half * FP + focal
            spectrum = jnp.concatenate(
                [spectra[pl.ds(first + i, NF, stride=16), :].astype(BF16) for i in range(wide)], axis=1
            )
            spectrum = jnp.concatenate([spectrum, spectrum], axis=0)
            signal = jnp.dot(inverse, spectrum, preferred_element_type=F32)
            limit = jnp.concatenate([onset[focal + i : focal + i + 1, lanes] for i in range(wide)], axis=1)
            lag = lax.broadcasted_iota(jnp.int32, signal.shape, 0)
            signal = jnp.where(lag < limit, signal, 0.0)
            signal = jnp.concatenate(high_low(signal), axis=0)
            result = jnp.dot(forward, signal, preferred_element_type=F32)
            result = result[:8] + result[8:]
            for i in range(wide):
                block = result[:, i * LANES : (i + 1) * LANES]
                mine[pl.ds(first + i, 4, stride=16), :] = block[:4]
                other[pl.ds(first + i, 4, stride=16), :] = block[4:]
    if owned:
        (owned,) = owned
        for owner in range(OWNERS):
            start = owner * stride + SHARED
            spectra[owner * PIECES : (owner + 1) * PIECES, :] = blocks[start : start + PIECES, :].astype(F32)
        for bin_ in range(4):
            high, low = (spectra[pl.ds(bin_ + 4 * i, OWNERS, stride=PIECES), :] for i in range(2))
            owned[pl.ds(bin_, OWNERS, stride=4), :] = high + low


def minus_roundtrip(rounded, own, onset, blocks, carried):
    stride = SHARED + PIECES if carried else SHARED
    out_shape = [jax.ShapeDtypeStruct((SHARED, LANES), F32)] * 2
    if carried:
        out_shape.append(jax.ShapeDtypeStruct((NF, LANES), F32))
    return pl.pallas_call(
        functools.partial(minus_kernel, stride),
        out_shape=out_shape,
        in_specs=[VMEM] * 4,
        out_specs=[VMEM] * len(out_shape),
        scratch_shapes=[pltpu.VMEM((OWNERS * SHARED, LANES), F32)],
        compiler_params=PARAMS,
        name="minus_roundtrip",
    )(rounded, own, onset, blocks)


def adjoint_kernel(mine, other, response, near, far, minus, held):
    lower = lax.axis_index("freq") < OWNERS // 2
    tiles = response.shape[3] // (2 * LANES)
    for bin_ in range(response.shape[1]):
        here, there = (
            jnp.concatenate([part[start : start + FP, :] for start in (bin_ * 16, bin_ * 16 + FP)], axis=1)
            for part in (mine, other)
        )
        both = jnp.where(lower, here, there), jnp.where(lower, there, here)
        for part in range(2):
            minus[part, bin_] = both[part]
        stacked = jnp.concatenate(both, axis=0).astype(BF16)
        first = jnp.dot(stacked, response[0, bin_], preferred_element_type=F32)
        second = jnp.dot(stacked, response[1, bin_], preferred_element_type=F32)
        parts = (first[:FP] + second[FP:], first[FP:] - second[:FP])
        for tile in range(tiles):
            for half in range(2):
                lane = (tile * 2 + half) * LANES
                for part in range(2):
                    start = (tile % 2 * tiles // 2 + tile // 2) * NF + (half * 2 + part) * 4 + bin_
                    held[pl.ds(start, FP, stride=16), :] = parts[part][:, lane : lane + LANES]
    core = lax.axis_index("core")
    rows = near.shape[0]
    near[...] = held[pl.ds(pl.multiple_of(core * rows, rows), rows), :]
    far[...] = held[pl.ds(pl.multiple_of((1 - core) * rows, rows), rows), :].astype(far.dtype)


def adjoint_product(mine, other, response):
    bins, receivers, sources = response.shape[1:]
    rows = NF * sources // (2 * LANES)
    return pl.pallas_call(
        adjoint_kernel,
        out_shape=(
            jax.ShapeDtypeStruct((rows // 2, LANES), F32),
            jax.ShapeDtypeStruct((rows // 2, LANES), BF16),
            jax.ShapeDtypeStruct((2, bins, FP, receivers), F32),
        ),
        in_specs=[VMEM] * 3,
        out_specs=(VMEM, VMEM, VMEM),
        scratch_shapes=[pltpu.VMEM((rows, LANES), F32)],
        compiler_params=PARAMS,
        name="adjoint_product",
    )(mine, other, in_vmem(response))


def add_kernel(near, far, out):
    out[...] = (near[...] + far[...].astype(F32)).astype(out.dtype)


def add(near, far):
    return pl.pallas_call(
        add_kernel,
        out_shape=jax.ShapeDtypeStruct(near.shape, BF16),
        in_specs=[VMEM, VMEM],
        out_specs=VMEM,
        compiler_params=PARAMS,
        name="add",
    )(near, far)


def plus_kernel(inverse, forward, onset, blocks, direct, out):
    device = lax.axis_index("freq")
    part, own_half, own_focal = device & 1, (device >> 1) & 1, device >> 2
    spectrum = blocks[:NF, :].astype(F32)
    for tile in range(1, blocks.shape[0] // NF):
        spectrum += blocks[tile * NF : (tile + 1) * NF, :].astype(F32)
    signal = jnp.dot(inverse[part], pieces(spectrum), preferred_element_type=F32)
    limits = jnp.where(own_half == 0, onset[:, :LANES], onset[:, LANES:])
    focal = lax.broadcasted_iota(jnp.int32, limits.shape, 0)
    limit = jnp.sum(jnp.where(focal == own_focal, limits, 0), axis=0, keepdims=True)
    lag = lax.broadcasted_iota(jnp.int32, signal.shape, 0)
    signal = jnp.where(lag < limit, signal, 0.0)
    result = jnp.dot(forward[part], pieces(signal), preferred_element_type=F32)
    result = (direct[...] + result).astype(out.dtype)
    for copy in range(out.shape[0] // NF):
        out[copy * NF : (copy + 1) * NF, :] = result


def plus_roundtrip(inverse, forward, onset, blocks, direct, copies, dtype):
    return pl.pallas_call(
        plus_kernel,
        out_shape=jax.ShapeDtypeStruct((copies * NF, LANES), dtype),
        in_specs=[VMEM] * 5,
        out_specs=VMEM,
        compiler_params=PARAMS,
        name="plus_roundtrip",
    )(inverse, forward, onset, blocks, direct)


def finish_kernel(blocks, out):
    for bin_ in range(out.shape[1]):
        for part in range(2):
            for half in range(2):
                value = blocks[pl.ds((half * 2 + part) * 4 + bin_, FP, stride=16), :]
                out[part, bin_, :, half * LANES : (half + 1) * LANES] = value


def finish(blocks, shape):
    return pl.pallas_call(
        finish_kernel,
        out_shape=jax.ShapeDtypeStruct(shape, F32),
        in_specs=[VMEM],
        out_specs=VMEM,
        compiler_params=PARAMS,
        name="finish",
    )(blocks)


def exchange(blocks, axes, count):
    shaped = blocks.reshape(count, blocks.shape[0] // count, LANES)
    return lax.all_to_all(shaped, axes, 0, 0, tiled=True).reshape(blocks.shape)


def on_device(response, direct, onset):
    groups, pairs = lax.axis_size("freq"), lax.axis_size("pair")
    rounded, own_bins, inverse, forward = (jnp.asarray(table) for table in tables())
    other_core = functools.partial(lax.ppermute, axis_name="core", perm=[(0, 1), (1, 0)])
    partners = [(owner, owner ^ (OWNERS // 2)) for owner in range(OWNERS)]
    shifted = [prepare(direct)]
    for shift in range(1, pairs):
        perm = [(pair, (pair + shift) % pairs) for pair in range(pairs)]
        shifted.append(lax.ppermute(shifted[0], "pair", perm))
    held = hold(response)
    mine = order(shifted, held)
    other = other_core(mine)
    for step in range(ITERS):
        if step == 0:
            upgoing = first_forward(mine, other, direct, held)
        else:
            upgoing = forward_product(mine, other, held)
        upgoing = exchange(upgoing, "freq", groups)
        mine, other, *owned = minus_roundtrip(rounded, own_bins, onset, upgoing, step == 0)
        if step == 0:
            (direct_columns,) = owned
        near, far, minus = adjoint_product(mine, lax.ppermute(other, "freq", partners), held)
        partial = exchange(add(near, other_core(far)), ("pair", "freq"), pairs * groups)
        last = step + 1 == ITERS
        copies, dtype = (1, F32) if last else (pairs, BF16)
        plus = plus_roundtrip(inverse, forward, onset, partial, direct_columns, copies, dtype)
        if last:
            plus = finish(exchange(plus, "freq", groups), direct.shape)
        else:
            mine = exchange(plus, ("pair", "freq"), pairs * groups)
            other = other_core(mine)
    return (minus, plus)


def solution(mesh):
    groups, tiles = mesh.devices.shape
    devices = mesh.devices.reshape(groups, tiles // 2, 2)
    tile = ("pair", "core")
    return jax.shard_map(
        on_device,
        mesh=jax.sharding.Mesh(devices, ("freq",) + tile),
        in_specs=(P(None, "freq", tile, None), P(None, "freq", None, tile), P(None, tile)),
        out_specs=(P(None, "freq", None, tile), P(None, "freq", None, tile)),
        check_vma=False,
    )
```

```python
import functools
import math

import jax
import jax.numpy as jnp
import numpy as np
from jax import lax
from jax.experimental import pallas as pl
from jax.experimental.pallas import tpu as pltpu
from jax.sharding import PartitionSpec as P

NT = 512
ITERS = 2
FIRST_BIN = 16
NF = 128
FP = 8
LAGS = 224
LANES = 128
BF16 = jnp.bfloat16
F32 = jnp.float32
VMEM_LIMIT = 24 * 1024 * 1024

SHARED = 64
PIECES = 16
OWNERS = 32


def split(table):
    high = table.astype(np.float32).astype(jnp.bfloat16)
    low = (table - high.astype(np.float64)).astype(np.float32).astype(jnp.bfloat16)
    return high, low


def tables():
    bins = FIRST_BIN + np.arange(NF)
    lags = np.arange(LAGS)
    angle = 2.0 * math.pi / NT * ((lags[:, None] * bins[None, :]) % NT)
    weight = np.where(lags == 0, 2.0 / NT, 4.0 / NT)
    rounded, inverse, forward, own = [], [], [], []
    devices = np.arange(OWNERS)
    pair = np.stack([devices, devices ^ (OWNERS // 2)], axis=1)
    for table in (np.cos(angle), np.sin(angle)):
        high, low = split(table)
        rounded.append(np.concatenate([high, low], axis=1))
        inverse.append(np.concatenate([high, high, low], axis=1))
        high, low = split((table * weight[:, None]).T)
        forward.append(np.concatenate([high, high, low], axis=1))
        high, low = (piece.reshape(OWNERS, 4, LAGS)[pair].reshape(OWNERS, 8, LAGS) for piece in (high, low))
        rows = np.concatenate(
            [np.concatenate([high, high], axis=2), np.concatenate([low, np.zeros_like(low)], axis=2)], axis=1
        )
        own.append(rows)
    return np.stack(rounded), np.stack(own, axis=1), np.stack(inverse), np.stack(forward)


def high_low(value):
    high = value.astype(BF16)
    return high, (value - high.astype(F32)).astype(BF16)


def pieces(value):
    high, low = high_low(value)
    return jnp.concatenate([high, low, high], axis=0)


def in_vmem(array):
    return pltpu.with_memory_space_constraint(array, pltpu.VMEM)


def in_hbm(array):
    return pltpu.with_memory_space_constraint(array, pltpu.HBM)


VMEM = pl.BlockSpec(memory_space=pltpu.VMEM)
HBM = pl.BlockSpec(memory_space=pltpu.HBM)
PARAMS = pltpu.CompilerParams(vmem_limit_bytes=VMEM_LIMIT)


def hold_kernel(direct, response, kept, pieces, near, held, done, near_done):
    fetch = pltpu.make_async_copy(direct, near, near_done)
    fetch.start()
    copy = pltpu.make_async_copy(response, kept, done)
    copy.start()
    fetch.wait()
    spread_direct(near, held, pieces)
    copy.wait()


def hold(direct, response):
    return pl.pallas_call(
        hold_kernel,
        out_shape=(
            pltpu.VMEM(response.shape, response.dtype),
            jax.ShapeDtypeStruct((OWNERS * PIECES, LANES), BF16),
        ),
        in_specs=[HBM, HBM],
        out_specs=(VMEM, VMEM),
        scratch_shapes=[
            pltpu.VMEM(direct.shape, F32),
            pltpu.VMEM((OWNERS * PIECES, LANES), F32),
            pltpu.SemaphoreType.DMA,
            pltpu.SemaphoreType.DMA,
        ],
        compiler_params=PARAMS,
        cost_estimate=pl.CostEstimate(flops=0, bytes_accessed=4 * response.size, transcendentals=0),
        name="hold",
    )(in_hbm(direct), in_hbm(response))


def prepare_kernel(direct, out):
    for bin_ in range(direct.shape[1]):
        out[bin_] = jnp.concatenate([direct[0, bin_], direct[1, bin_]], axis=0).astype(BF16)


def prepare(direct):
    parts, bins, focal, positions = direct.shape
    return pl.pallas_call(
        prepare_kernel,
        out_shape=jax.ShapeDtypeStruct((bins, parts * focal, positions), BF16),
        in_specs=[VMEM],
        out_specs=VMEM,
        compiler_params=PARAMS,
        name="prepare",
    )(direct)


def order_kernel(*refs):
    *shifted, _, out = refs
    pairs = len(shifted)
    for shift in range(pairs):
        out[(lax.axis_index("pair") - shift + pairs) & (pairs - 1)] = shifted[shift][...]


def order(shifted, held):
    return pl.pallas_call(
        order_kernel,
        out_shape=jax.ShapeDtypeStruct((len(shifted),) + shifted[0].shape, BF16),
        in_specs=[VMEM] * (len(shifted) + 1),
        out_specs=VMEM,
        compiler_params=PARAMS,
        name="order",
    )(*shifted, in_vmem(held))


def forward_dots(blocks, response, bin_, core):
    dims = (((1,), (1,)), ((), ()))
    first = second = 0.0
    for pair, block in enumerate(blocks):
        width = block.shape[1]
        lanes = pl.ds(pl.multiple_of((2 * pair + core) * width, width), width)
        first += lax.dot_general(block, response[0, bin_, :, lanes], dims, preferred_element_type=F32)
        second += lax.dot_general(block, response[1, bin_, :, lanes], dims, preferred_element_type=F32)
    return jnp.concatenate([first[:FP] - second[FP:], first[FP:] + second[:FP]], axis=0)


def share(value, bin_, out, stride):
    value = value.astype(BF16)
    for owner in range(OWNERS):
        half = owner // (OWNERS // 2)
        start = owner * stride + bin_ * 16
        out[start : start + 16, :] = value[:, half * LANES : (half + 1) * LANES]


def spread_direct(direct, held, out):
    held[...] = jnp.zeros_like(held)
    for bin_ in range(direct.shape[1]):
        for half in range(2):
            for part in range(2):
                value = direct[part, bin_, :, half * LANES : (half + 1) * LANES]
                start = (half * 2 + part) * PIECES + bin_
                for row, piece in enumerate(high_low(value)):
                    held[pl.ds(start + 4 * row, FP, stride=4 * PIECES), :] = piece.astype(F32)
    out[...] = held[...].astype(BF16)


def near_direct_kernel(mine, response, out):
    pairs, bins = mine.shape[:2]
    core = lax.axis_index("core")
    for bin_ in range(bins):
        out[bin_] = forward_dots([mine[pair, bin_] for pair in range(pairs)], response, bin_, core)


def near_direct(mine, response):
    bins, receivers = response.shape[1:3]
    return pl.pallas_call(
        near_direct_kernel,
        out_shape=jax.ShapeDtypeStruct((bins, 2 * FP, receivers), F32),
        in_specs=[VMEM] * 2,
        out_specs=VMEM,
        compiler_params=PARAMS,
        name="near_direct",
    )(mine, in_vmem(response))


def far_direct_kernel(other, near, pieces, response, out):
    stride = SHARED + PIECES
    for owner in range(OWNERS):
        start = owner * stride + SHARED
        out[start : start + PIECES, :] = pieces[owner * PIECES : (owner + 1) * PIECES, :]
    pairs, bins = other.shape[:2]
    core = 1 - lax.axis_index("core")
    for bin_ in range(bins):
        value = forward_dots([other[pair, bin_] for pair in range(pairs)], response, bin_, core)
        share(near[bin_] + value, bin_, out, stride)


def far_direct(other, near, pieces, response):
    return pl.pallas_call(
        far_direct_kernel,
        out_shape=jax.ShapeDtypeStruct((OWNERS * (SHARED + PIECES), LANES), BF16),
        in_specs=[VMEM] * 4,
        out_specs=VMEM,
        compiler_params=PARAMS,
        name="far_direct",
    )(other, near, pieces, in_vmem(response))


def columns_of(held, bin_):
    blocks = []
    for pair in range(held.shape[0] // NF):
        halves = []
        for half in range(2):
            start = pair * NF + half * 8 + bin_
            both = [held[pl.ds(start + part * 4, FP, stride=16), :] for part in range(2)]
            halves.append(jnp.concatenate(both, axis=0))
        blocks.append(jnp.concatenate(halves, axis=1).astype(BF16))
    return blocks


def near_forward_kernel(mine, response, out, held):
    held[...] = mine[...].astype(F32)
    core = lax.axis_index("core")
    for bin_ in range(response.shape[1]):
        out[bin_] = forward_dots(columns_of(held, bin_), response, bin_, core)


def near_forward(mine, response):
    bins, receivers = response.shape[1:3]
    return pl.pallas_call(
        near_forward_kernel,
        out_shape=jax.ShapeDtypeStruct((bins, 2 * FP, receivers), F32),
        in_specs=[VMEM] * 2,
        out_specs=VMEM,
        scratch_shapes=[pltpu.VMEM(mine.shape, F32)],
        compiler_params=PARAMS,
        name="near_forward",
    )(mine, in_vmem(response))


def far_forward_kernel(other, near, response, out, held):
    held[...] = other[...].astype(F32)
    core = 1 - lax.axis_index("core")
    for bin_ in range(response.shape[1]):
        value = forward_dots(columns_of(held, bin_), response, bin_, core)
        share(near[bin_] + value, bin_, out, SHARED)


def far_forward(other, near, response):
    return pl.pallas_call(
        far_forward_kernel,
        out_shape=jax.ShapeDtypeStruct((OWNERS * SHARED, LANES), BF16),
        in_specs=[VMEM] * 3,
        out_specs=VMEM,
        scratch_shapes=[pltpu.VMEM(other.shape, F32)],
        compiler_params=PARAMS,
        name="far_forward",
    )(other, near, in_vmem(response))


def minus_kernel(stride, rounded, own, onset, blocks, mine, other, *refs):
    *owned, spectra = refs
    for owner in range(OWNERS):
        start = owner * stride
        spectra[owner * SHARED : (owner + 1) * SHARED, :] = blocks[start : start + SHARED, :].astype(F32)
    device = lax.axis_index("freq")
    limits = jnp.where(device < OWNERS // 2, onset[:, :LANES], onset[:, LANES:])
    wide = 2
    for part in range(2):
        for focal in range(0, FP, wide):
            first = part * FP + focal
            spectrum = jnp.concatenate(
                [spectra[pl.ds(first + i, NF, stride=16), :].astype(BF16) for i in range(wide)], axis=1
            )
            spectrum = jnp.concatenate([spectrum, spectrum], axis=0)
            signal = jnp.dot(rounded[part], spectrum, preferred_element_type=F32)
            limit = jnp.concatenate([limits[focal + i : focal + i + 1, :] for i in range(wide)], axis=1)
            lag = lax.broadcasted_iota(jnp.int32, signal.shape, 0)
            signal = jnp.where(lag < limit, signal, 0.0)
            signal = jnp.concatenate(high_low(signal), axis=0)
            result = jnp.dot(own[device, part], signal, preferred_element_type=F32)
            result = result[:8] + result[8:]
            for i in range(wide):
                block = result[:, i * LANES : (i + 1) * LANES]
                mine[pl.ds(first + i, 4, stride=16), :] = block[:4]
                other[pl.ds(first + i, 4, stride=16), :] = block[4:]
    if owned:
        (owned,) = owned
        for owner in range(OWNERS):
            start = owner * stride + SHARED
            spectra[owner * PIECES : (owner + 1) * PIECES, :] = blocks[start : start + PIECES, :].astype(F32)
        for bin_ in range(4):
            high, low = (spectra[pl.ds(bin_ + 4 * i, OWNERS, stride=PIECES), :] for i in range(2))
            owned[pl.ds(bin_, OWNERS, stride=4), :] = high + low


def minus_roundtrip(rounded, own, onset, blocks, carried):
    stride = SHARED + PIECES if carried else SHARED
    out_shape = [jax.ShapeDtypeStruct((SHARED, LANES), F32)] * 2
    if carried:
        out_shape.append(jax.ShapeDtypeStruct((NF, LANES), F32))
    return pl.pallas_call(
        functools.partial(minus_kernel, stride),
        out_shape=out_shape,
        in_specs=[VMEM] * 4,
        out_specs=[VMEM] * len(out_shape),
        scratch_shapes=[pltpu.VMEM((OWNERS * SHARED, LANES), F32)],
        compiler_params=PARAMS,
        name="minus_roundtrip",
    )(rounded, own, onset, blocks)


def adjoint_dots(block, response, bin_, half, core, held, start):
    receivers, sources = response.shape[2:]
    rows = pl.ds(pl.multiple_of(half * LANES, LANES), LANES)
    width = 2 * LANES
    for pair in range(sources // (2 * width)):
        lanes = pl.ds(pl.multiple_of((2 * pair + core) * width, width), width)
        first = jnp.dot(block, response[0, bin_, rows, lanes], preferred_element_type=F32)
        second = jnp.dot(block, response[1, bin_, rows, lanes], preferred_element_type=F32)
        parts = (first[:FP] + second[FP:], first[FP:] - second[:FP])
        for side in range(2):
            for part in range(2):
                row = start + pair * NF + (side * 2 + part) * 4 + bin_
                held[pl.ds(row, FP, stride=16), :] = parts[part][:, side * LANES : (side + 1) * LANES]


def first_half_kernel(mine, response, out):
    half = lax.axis_index("freq") >> 4
    core = lax.axis_index("core")
    for bin_ in range(response.shape[1]):
        block = mine[bin_ * 16 : (bin_ + 1) * 16, :].astype(BF16)
        adjoint_dots(block, response, bin_, half, core, out, 0)
        adjoint_dots(block, response, bin_, half, 1 - core, out, out.shape[0] // 2)


def first_half(mine, response):
    rows = NF * response.shape[3] // (2 * LANES)
    return pl.pallas_call(
        first_half_kernel,
        out_shape=jax.ShapeDtypeStruct((rows, LANES), F32),
        in_specs=[VMEM] * 2,
        out_specs=VMEM,
        compiler_params=PARAMS,
        name="first_half",
    )(mine, in_vmem(response))


def far_half_kernel(other, partial, response, out, held):
    half = 1 - (lax.axis_index("freq") >> 4)
    core = 1 - lax.axis_index("core")
    for bin_ in range(response.shape[1]):
        block = other[bin_ * 16 : (bin_ + 1) * 16, :].astype(BF16)
        adjoint_dots(block, response, bin_, half, core, held, 0)
    out[...] = (held[...] + partial[held.shape[0] :, :]).astype(out.dtype)


def far_half(other, partial, response):
    rows = partial.shape[0] // 2
    return pl.pallas_call(
        far_half_kernel,
        out_shape=jax.ShapeDtypeStruct((rows, LANES), BF16),
        in_specs=[VMEM] * 3,
        out_specs=VMEM,
        scratch_shapes=[pltpu.VMEM((rows, LANES), F32)],
        compiler_params=PARAMS,
        name="far_half",
    )(other, partial, in_vmem(response))


def near_half_kernel(mine, other, partial, response, out, *refs):
    *minus, held = refs
    half = lax.axis_index("freq") >> 4
    core = lax.axis_index("core")
    for bin_ in range(response.shape[1]):
        block = other[bin_ * 16 : (bin_ + 1) * 16, :].astype(BF16)
        adjoint_dots(block, response, bin_, 1 - half, core, held, 0)
        for part in range(2):
            rows = slice(bin_ * 16 + part * FP, bin_ * 16 + (part + 1) * FP)
            for place, source in ((half, mine), (1 - half, other)):
                lanes = pl.ds(pl.multiple_of(place * LANES, LANES), LANES)
                for spectrum in minus:
                    spectrum[part, bin_, :, lanes] = source[rows, :]
    out[...] = held[...] + partial[: held.shape[0], :]


def near_half(mine, other, partial, response, last):
    rows = partial.shape[0] // 2
    out_shape = [jax.ShapeDtypeStruct((rows, LANES), F32)]
    if last:
        out_shape.append(jax.ShapeDtypeStruct((2, response.shape[1], FP, response.shape[2]), F32))
    return pl.pallas_call(
        near_half_kernel,
        out_shape=out_shape,
        in_specs=[VMEM] * 4,
        out_specs=[VMEM] * len(out_shape),
        scratch_shapes=[pltpu.VMEM((rows, LANES), F32)],
        compiler_params=PARAMS,
        name="near_half",
    )(mine, other, partial, in_vmem(response))


def add_kernel(near, far, out):
    out[...] = (near[...] + far[...].astype(F32)).astype(out.dtype)


def add(near, far):
    return pl.pallas_call(
        add_kernel,
        out_shape=jax.ShapeDtypeStruct(near.shape, BF16),
        in_specs=[VMEM, VMEM],
        out_specs=VMEM,
        compiler_params=PARAMS,
        name="add",
    )(near, far)


def plus_kernel(inverse, forward, onset, blocks, direct, out):
    device = lax.axis_index("freq")
    part, own_half, own_focal = device & 1, (device >> 1) & 1, device >> 2
    spectrum = blocks[:NF, :].astype(F32)
    for tile in range(1, blocks.shape[0] // NF):
        spectrum += blocks[tile * NF : (tile + 1) * NF, :].astype(F32)
    signal = jnp.dot(inverse[part], pieces(spectrum), preferred_element_type=F32)
    limits = jnp.where(own_half == 0, onset[:, :LANES], onset[:, LANES:])
    focal = lax.broadcasted_iota(jnp.int32, limits.shape, 0)
    limit = jnp.sum(jnp.where(focal == own_focal, limits, 0), axis=0, keepdims=True)
    lag = lax.broadcasted_iota(jnp.int32, signal.shape, 0)
    signal = jnp.where(lag < limit, signal, 0.0)
    result = jnp.dot(forward[part], pieces(signal), preferred_element_type=F32)
    result = (direct[...] + result).astype(out.dtype)
    for copy in range(out.shape[0] // NF):
        out[copy * NF : (copy + 1) * NF, :] = result


def plus_roundtrip(inverse, forward, onset, blocks, direct, copies, dtype):
    return pl.pallas_call(
        plus_kernel,
        out_shape=jax.ShapeDtypeStruct((copies * NF, LANES), dtype),
        in_specs=[VMEM] * 5,
        out_specs=VMEM,
        compiler_params=PARAMS,
        name="plus_roundtrip",
    )(inverse, forward, onset, blocks, direct)


def finish_kernel(blocks, out):
    for bin_ in range(out.shape[1]):
        for part in range(2):
            for half in range(2):
                value = blocks[pl.ds((half * 2 + part) * 4 + bin_, FP, stride=16), :]
                out[part, bin_, :, half * LANES : (half + 1) * LANES] = value


def finish(blocks, shape):
    return pl.pallas_call(
        finish_kernel,
        out_shape=jax.ShapeDtypeStruct(shape, F32),
        in_specs=[VMEM],
        out_specs=VMEM,
        compiler_params=PARAMS,
        name="finish",
    )(blocks)


def exchange(blocks, axes, count):
    shaped = blocks.reshape(count, blocks.shape[0] // count, LANES)
    return lax.all_to_all(shaped, axes, 0, 0, tiled=True).reshape(blocks.shape)


def on_device(response, direct, onset):
    groups, pairs = lax.axis_size("freq"), lax.axis_size("pair")
    rounded, own_bins, inverse, forward = (jnp.asarray(table) for table in tables())
    other_core = functools.partial(lax.ppermute, axis_name="core", perm=[(0, 1), (1, 0)])
    partners = [(owner, owner ^ (OWNERS // 2)) for owner in range(OWNERS)]
    shifted = [prepare(direct)]
    for shift in range(1, pairs):
        perm = [(pair, (pair + shift) % pairs) for pair in range(pairs)]
        shifted.append(lax.ppermute(shifted[0], "pair", perm))
    held, sent = hold(direct, response)
    mine = order(shifted, held)
    other = other_core(mine)
    for step in range(ITERS):
        if step == 0:
            upgoing = far_direct(other, near_direct(mine, held), sent, held)
        else:
            upgoing = far_forward(other, near_forward(mine, held), held)
        upgoing = exchange(upgoing, "freq", groups)
        mine, other, *owned = minus_roundtrip(rounded, own_bins, onset, upgoing, step == 0)
        if step == 0:
            (direct_columns,) = owned
        other = lax.ppermute(other, "freq", partners)
        partial = first_half(mine, held)
        far = far_half(other, partial, held)
        last = step + 1 == ITERS
        near, *minus = near_half(mine, other, partial, held, last)
        partial = exchange(add(near, other_core(far)), ("pair", "freq"), pairs * groups)
        copies, dtype = (1, F32) if last else (pairs, BF16)
        plus = plus_roundtrip(inverse, forward, onset, partial, direct_columns, copies, dtype)
        if last:
            plus = finish(exchange(plus, "freq", groups), direct.shape)
        else:
            mine = exchange(plus, ("pair", "freq"), pairs * groups)
            other = other_core(mine)
    return (minus[0], plus)


def solution(mesh):
    groups, tiles = mesh.devices.shape
    devices = mesh.devices.reshape(groups, tiles // 2, 2)
    tile = ("pair", "core")
    return jax.shard_map(
        on_device,
        mesh=jax.sharding.Mesh(devices, ("freq",) + tile),
        in_specs=(P(None, "freq", tile, None), P(None, "freq", None, tile), P(None, tile)),
        out_specs=(P(None, "freq", None, tile), P(None, "freq", None, tile)),
        check_vma=False,
    )
```

```python
import functools
import math

import jax
import jax.numpy as jnp
import numpy as np
from jax import lax
from jax.experimental import pallas as pl
from jax.experimental.pallas import tpu as pltpu
from jax.sharding import PartitionSpec as P

NT = 512
ITERS = 2
FIRST_BIN = 16
NF = 128
FP = 8
LAGS = 224
LANES = 128
BF16 = jnp.bfloat16
F32 = jnp.float32
VMEM_LIMIT = 10 * 1024 * 1024

SHARED = 64
PIECES = 16
OWNERS = 32


def split(table):
    high = table.astype(np.float32).astype(jnp.bfloat16)
    low = (table - high.astype(np.float64)).astype(np.float32).astype(jnp.bfloat16)
    return high, low


def tables():
    bins = FIRST_BIN + np.arange(NF)
    lags = np.arange(LAGS)
    angle = 2.0 * math.pi / NT * ((lags[:, None] * bins[None, :]) % NT)
    weight = np.where(lags == 0, 2.0 / NT, 4.0 / NT)
    rounded, inverse, forward, own = [], [], [], []
    devices = np.arange(OWNERS)
    pair = np.stack([devices, devices ^ (OWNERS // 2)], axis=1)
    for table in (np.cos(angle), np.sin(angle)):
        high, low = split(table)
        rounded.append(np.concatenate([high, low], axis=1))
        inverse.append(np.concatenate([high, high, low], axis=1))
        high, low = split((table * weight[:, None]).T)
        forward.append(np.concatenate([high, high, low], axis=1))
        high, low = (piece.reshape(OWNERS, 4, LAGS)[pair].reshape(OWNERS, 8, LAGS) for piece in (high, low))
        rows = np.concatenate(
            [np.concatenate([high, high], axis=2), np.concatenate([low, np.zeros_like(low)], axis=2)], axis=1
        )
        own.append(rows)
    return np.stack(rounded), np.stack(own, axis=1), np.stack(inverse), np.stack(forward)


def high_low(value):
    high = value.astype(BF16)
    return high, (value - high.astype(F32)).astype(BF16)


def pieces(value):
    high, low = high_low(value)
    return jnp.concatenate([high, low, high], axis=0)


def in_vmem(array):
    return pltpu.with_memory_space_constraint(array, pltpu.VMEM)


def in_hbm(array):
    return pltpu.with_memory_space_constraint(array, pltpu.HBM)


VMEM = pl.BlockSpec(memory_space=pltpu.VMEM)
HBM = pl.BlockSpec(memory_space=pltpu.HBM)
PARAMS = pltpu.CompilerParams(vmem_limit_bytes=VMEM_LIMIT)


def hold_kernel(direct, response, kept, turned, pieces, near, held, done, near_done):
    copies = [
        pltpu.make_async_copy(response.at[part, bin_], kept.at[part, bin_], done.at[part, bin_])
        for bin_ in range(response.shape[1])
        for part in range(2)
    ]
    ahead = 4
    fetch = pltpu.make_async_copy(direct, near, near_done)
    copies[0].start()
    fetch.start()
    for copy in copies[1:ahead]:
        copy.start()
    fetch.wait()
    spread_direct(near, held, pieces)
    for step, copy in enumerate(copies):
        copy.wait()
        for later in copies[step + ahead : step + ahead + 1]:
            later.start()
        part, bin_ = step % 2, step // 2
        turned[part, bin_] = kept[part, bin_].T


def hold(direct, response):
    parts, bins, receivers, sources = response.shape
    return pl.pallas_call(
        hold_kernel,
        out_shape=(
            pltpu.VMEM(response.shape, response.dtype),
            pltpu.VMEM((parts, bins, sources, receivers), response.dtype),
            jax.ShapeDtypeStruct((OWNERS * PIECES, LANES), BF16),
        ),
        in_specs=[HBM, HBM],
        out_specs=(VMEM, VMEM, VMEM),
        scratch_shapes=[
            pltpu.VMEM(direct.shape, F32),
            pltpu.VMEM((OWNERS * PIECES, LANES), F32),
            pltpu.SemaphoreType.DMA((parts, bins)),
            pltpu.SemaphoreType.DMA,
        ],
        compiler_params=PARAMS,
        cost_estimate=pl.CostEstimate(flops=0, bytes_accessed=4 * response.size, transcendentals=0),
        name="hold",
    )(in_hbm(direct), in_hbm(response))


def prepare_kernel(direct, out):
    for bin_ in range(direct.shape[1]):
        out[bin_] = jnp.concatenate([direct[0, bin_], direct[1, bin_]], axis=0).astype(BF16)


def prepare(direct):
    parts, bins, focal, positions = direct.shape
    return pl.pallas_call(
        prepare_kernel,
        out_shape=jax.ShapeDtypeStruct((bins, parts * focal, positions), BF16),
        in_specs=[VMEM],
        out_specs=VMEM,
        compiler_params=PARAMS,
        name="prepare",
    )(direct)


def order_kernel(*refs):
    *shifted, _, out = refs
    pairs = len(shifted)
    for shift in range(pairs):
        out[(lax.axis_index("pair") - shift + pairs) & (pairs - 1)] = shifted[shift][...]


def order(shifted, held):
    return pl.pallas_call(
        order_kernel,
        out_shape=jax.ShapeDtypeStruct((len(shifted),) + shifted[0].shape, BF16),
        in_specs=[VMEM] * (len(shifted) + 1),
        out_specs=VMEM,
        compiler_params=PARAMS,
        name="order",
    )(*shifted, in_vmem(held))


def forward_dots(blocks, turned, bin_, core):
    first = second = 0.0
    for pair, block in enumerate(blocks):
        width = block.shape[1]
        rows = pl.ds(pl.multiple_of((2 * pair + core) * width, width), width)
        first += jnp.dot(block, turned[0, bin_, rows, :], preferred_element_type=F32)
        second += jnp.dot(block, turned[1, bin_, rows, :], preferred_element_type=F32)
    return jnp.concatenate([first[:FP] - second[FP:], first[FP:] + second[:FP]], axis=0)


def share(value, bin_, out, stride):
    value = value.astype(BF16)
    for owner in range(OWNERS):
        half = owner // (OWNERS // 2)
        start = owner * stride + bin_ * 16
        out[start : start + 16, :] = value[:, half * LANES : (half + 1) * LANES]


def spread_direct(direct, held, out):
    held[...] = jnp.zeros_like(held)
    for bin_ in range(direct.shape[1]):
        for half in range(2):
            for part in range(2):
                value = direct[part, bin_, :, half * LANES : (half + 1) * LANES]
                start = (half * 2 + part) * PIECES + bin_
                for row, piece in enumerate(high_low(value)):
                    held[pl.ds(start + 4 * row, FP, stride=4 * PIECES), :] = piece.astype(F32)
    out[...] = held[...].astype(BF16)


def near_direct_kernel(mine, turned, out):
    pairs, bins = mine.shape[:2]
    core = lax.axis_index("core")
    for bin_ in range(bins):
        out[bin_] = forward_dots([mine[pair, bin_] for pair in range(pairs)], turned, bin_, core)


def near_direct(mine, turned):
    bins, _, receivers = turned.shape[1:]
    return pl.pallas_call(
        near_direct_kernel,
        out_shape=jax.ShapeDtypeStruct((bins, 2 * FP, receivers), F32),
        in_specs=[VMEM] * 2,
        out_specs=VMEM,
        compiler_params=PARAMS,
        name="near_direct",
    )(mine, in_vmem(turned))


def far_direct_kernel(other, near, pieces, turned, out):
    stride = SHARED + PIECES
    for owner in range(OWNERS):
        start = owner * stride + SHARED
        out[start : start + PIECES, :] = pieces[owner * PIECES : (owner + 1) * PIECES, :]
    pairs, bins = other.shape[:2]
    core = 1 - lax.axis_index("core")
    for bin_ in range(bins):
        value = forward_dots([other[pair, bin_] for pair in range(pairs)], turned, bin_, core)
        share(near[bin_] + value, bin_, out, stride)


def far_direct(other, near, pieces, turned):
    return pl.pallas_call(
        far_direct_kernel,
        out_shape=jax.ShapeDtypeStruct((OWNERS * (SHARED + PIECES), LANES), BF16),
        in_specs=[VMEM] * 4,
        out_specs=VMEM,
        compiler_params=PARAMS,
        name="far_direct",
    )(other, near, pieces, in_vmem(turned))


def columns_of(held, bin_):
    blocks = []
    for pair in range(held.shape[0] // NF):
        halves = []
        for half in range(2):
            start = pair * NF + half * 8 + bin_
            both = [held[pl.ds(start + part * 4, FP, stride=16), :] for part in range(2)]
            halves.append(jnp.concatenate(both, axis=0))
        blocks.append(jnp.concatenate(halves, axis=1).astype(BF16))
    return blocks


def near_forward_kernel(mine, turned, out, held):
    held[...] = mine[...].astype(F32)
    core = lax.axis_index("core")
    for bin_ in range(turned.shape[1]):
        out[bin_] = forward_dots(columns_of(held, bin_), turned, bin_, core)


def near_forward(mine, turned):
    bins, _, receivers = turned.shape[1:]
    return pl.pallas_call(
        near_forward_kernel,
        out_shape=jax.ShapeDtypeStruct((bins, 2 * FP, receivers), F32),
        in_specs=[VMEM] * 2,
        out_specs=VMEM,
        scratch_shapes=[pltpu.VMEM(mine.shape, F32)],
        compiler_params=PARAMS,
        name="near_forward",
    )(mine, in_vmem(turned))


def far_forward_kernel(other, near, turned, out, held):
    held[...] = other[...].astype(F32)
    core = 1 - lax.axis_index("core")
    for bin_ in range(turned.shape[1]):
        value = forward_dots(columns_of(held, bin_), turned, bin_, core)
        share(near[bin_] + value, bin_, out, SHARED)


def far_forward(other, near, turned):
    return pl.pallas_call(
        far_forward_kernel,
        out_shape=jax.ShapeDtypeStruct((OWNERS * SHARED, LANES), BF16),
        in_specs=[VMEM] * 3,
        out_specs=VMEM,
        scratch_shapes=[pltpu.VMEM(other.shape, F32)],
        compiler_params=PARAMS,
        name="far_forward",
    )(other, near, in_vmem(turned))


def minus_kernel(stride, rounded, own, onset, blocks, mine, other, *refs):
    *owned, spectra = refs
    for owner in range(OWNERS):
        start = owner * stride
        spectra[owner * SHARED : (owner + 1) * SHARED, :] = blocks[start : start + SHARED, :].astype(F32)
    device = lax.axis_index("freq")
    limits = jnp.where(device < OWNERS // 2, onset[:, :LANES], onset[:, LANES:])
    wide = 2
    for part in range(2):
        for focal in range(0, FP, wide):
            first = part * FP + focal
            spectrum = jnp.concatenate(
                [spectra[pl.ds(first + i, NF, stride=16), :].astype(BF16) for i in range(wide)], axis=1
            )
            spectrum = jnp.concatenate([spectrum, spectrum], axis=0)
            signal = jnp.dot(rounded[part], spectrum, preferred_element_type=F32)
            limit = jnp.concatenate([limits[focal + i : focal + i + 1, :] for i in range(wide)], axis=1)
            lag = lax.broadcasted_iota(jnp.int32, signal.shape, 0)
            signal = jnp.where(lag < limit, signal, 0.0)
            signal = jnp.concatenate(high_low(signal), axis=0)
            result = jnp.dot(own[device, part], signal, preferred_element_type=F32)
            result = result[:8] + result[8:]
            for i in range(wide):
                block = result[:, i * LANES : (i + 1) * LANES]
                mine[pl.ds(first + i, 4, stride=16), :] = block[:4]
                other[pl.ds(first + i, 4, stride=16), :] = block[4:]
    if owned:
        (owned,) = owned
        for owner in range(OWNERS):
            start = owner * stride + SHARED
            spectra[owner * PIECES : (owner + 1) * PIECES, :] = blocks[start : start + PIECES, :].astype(F32)
        for bin_ in range(4):
            high, low = (spectra[pl.ds(bin_ + 4 * i, OWNERS, stride=PIECES), :] for i in range(2))
            owned[pl.ds(bin_, OWNERS, stride=4), :] = high + low


def minus_roundtrip(rounded, own, onset, blocks, carried):
    stride = SHARED + PIECES if carried else SHARED
    out_shape = [jax.ShapeDtypeStruct((SHARED, LANES), F32)] * 2
    if carried:
        out_shape.append(jax.ShapeDtypeStruct((NF, LANES), F32))
    return pl.pallas_call(
        functools.partial(minus_kernel, stride),
        out_shape=out_shape,
        in_specs=[VMEM] * 4,
        out_specs=[VMEM] * len(out_shape),
        scratch_shapes=[pltpu.VMEM((OWNERS * SHARED, LANES), F32)],
        compiler_params=PARAMS,
        name="minus_roundtrip",
    )(rounded, own, onset, blocks)


def adjoint_dots(block, response, bin_, half, core, held, start):
    receivers, sources = response.shape[2:]
    rows = pl.ds(pl.multiple_of(half * LANES, LANES), LANES)
    width = 2 * LANES
    for pair in range(sources // (2 * width)):
        lanes = pl.ds(pl.multiple_of((2 * pair + core) * width, width), width)
        first = jnp.dot(block, response[0, bin_, rows, lanes], preferred_element_type=F32)
        second = jnp.dot(block, response[1, bin_, rows, lanes], preferred_element_type=F32)
        parts = (first[:FP] + second[FP:], first[FP:] - second[:FP])
        for side in range(2):
            for part in range(2):
                row = start + pair * NF + (side * 2 + part) * 4 + bin_
                held[pl.ds(row, FP, stride=16), :] = parts[part][:, side * LANES : (side + 1) * LANES]


def first_half_kernel(mine, response, out):
    half = lax.axis_index("freq") >> 4
    core = lax.axis_index("core")
    for bin_ in range(response.shape[1]):
        block = mine[bin_ * 16 : (bin_ + 1) * 16, :].astype(BF16)
        adjoint_dots(block, response, bin_, half, core, out, 0)
        adjoint_dots(block, response, bin_, half, 1 - core, out, out.shape[0] // 2)


def first_half(mine, response):
    rows = NF * response.shape[3] // (2 * LANES)
    return pl.pallas_call(
        first_half_kernel,
        out_shape=jax.ShapeDtypeStruct((rows, LANES), F32),
        in_specs=[VMEM] * 2,
        out_specs=VMEM,
        compiler_params=PARAMS,
        name="first_half",
    )(mine, in_vmem(response))


def far_half_kernel(other, partial, response, out, held):
    half = 1 - (lax.axis_index("freq") >> 4)
    core = 1 - lax.axis_index("core")
    for bin_ in range(response.shape[1]):
        block = other[bin_ * 16 : (bin_ + 1) * 16, :].astype(BF16)
        adjoint_dots(block, response, bin_, half, core, held, 0)
    out[...] = (held[...] + partial[held.shape[0] :, :]).astype(out.dtype)


def far_half(other, partial, response):
    rows = partial.shape[0] // 2
    return pl.pallas_call(
        far_half_kernel,
        out_shape=jax.ShapeDtypeStruct((rows, LANES), BF16),
        in_specs=[VMEM] * 3,
        out_specs=VMEM,
        scratch_shapes=[pltpu.VMEM((rows, LANES), F32)],
        compiler_params=PARAMS,
        name="far_half",
    )(other, partial, in_vmem(response))


def near_half_kernel(mine, other, partial, response, out, *refs):
    *minus, held = refs
    half = lax.axis_index("freq") >> 4
    core = lax.axis_index("core")
    for bin_ in range(response.shape[1]):
        block = other[bin_ * 16 : (bin_ + 1) * 16, :].astype(BF16)
        adjoint_dots(block, response, bin_, 1 - half, core, held, 0)
        for part in range(2):
            rows = slice(bin_ * 16 + part * FP, bin_ * 16 + (part + 1) * FP)
            for place, source in ((half, mine), (1 - half, other)):
                lanes = pl.ds(pl.multiple_of(place * LANES, LANES), LANES)
                for spectrum in minus:
                    spectrum[part, bin_, :, lanes] = source[rows, :]
    out[...] = held[...] + partial[: held.shape[0], :]


def near_half(mine, other, partial, response, last):
    rows = partial.shape[0] // 2
    out_shape = [jax.ShapeDtypeStruct((rows, LANES), F32)]
    if last:
        out_shape.append(jax.ShapeDtypeStruct((2, response.shape[1], FP, response.shape[2]), F32))
    return pl.pallas_call(
        near_half_kernel,
        out_shape=out_shape,
        in_specs=[VMEM] * 4,
        out_specs=[VMEM] * len(out_shape),
        scratch_shapes=[pltpu.VMEM((rows, LANES), F32)],
        compiler_params=PARAMS,
        name="near_half",
    )(mine, other, partial, in_vmem(response))


def add_kernel(near, far, out):
    out[...] = (near[...] + far[...].astype(F32)).astype(out.dtype)


def add(near, far):
    return pl.pallas_call(
        add_kernel,
        out_shape=jax.ShapeDtypeStruct(near.shape, BF16),
        in_specs=[VMEM, VMEM],
        out_specs=VMEM,
        compiler_params=PARAMS,
        name="add",
    )(near, far)


def plus_kernel(inverse, forward, onset, blocks, direct, out):
    device = lax.axis_index("freq")
    part, own_half, own_focal = device & 1, (device >> 1) & 1, device >> 2
    spectrum = blocks[:NF, :].astype(F32)
    for tile in range(1, blocks.shape[0] // NF):
        spectrum += blocks[tile * NF : (tile + 1) * NF, :].astype(F32)
    signal = jnp.dot(inverse[part], pieces(spectrum), preferred_element_type=F32)
    limits = jnp.where(own_half == 0, onset[:, :LANES], onset[:, LANES:])
    focal = lax.broadcasted_iota(jnp.int32, limits.shape, 0)
    limit = jnp.sum(jnp.where(focal == own_focal, limits, 0), axis=0, keepdims=True)
    lag = lax.broadcasted_iota(jnp.int32, signal.shape, 0)
    signal = jnp.where(lag < limit, signal, 0.0)
    result = jnp.dot(forward[part], pieces(signal), preferred_element_type=F32)
    result = (direct[...] + result).astype(out.dtype)
    for copy in range(out.shape[0] // NF):
        out[copy * NF : (copy + 1) * NF, :] = result


def plus_roundtrip(inverse, forward, onset, blocks, direct, copies, dtype):
    return pl.pallas_call(
        plus_kernel,
        out_shape=jax.ShapeDtypeStruct((copies * NF, LANES), dtype),
        in_specs=[VMEM] * 5,
        out_specs=VMEM,
        compiler_params=PARAMS,
        name="plus_roundtrip",
    )(inverse, forward, onset, blocks, direct)


def finish_kernel(blocks, out):
    for bin_ in range(out.shape[1]):
        for part in range(2):
            for half in range(2):
                value = blocks[pl.ds((half * 2 + part) * 4 + bin_, FP, stride=16), :]
                out[part, bin_, :, half * LANES : (half + 1) * LANES] = value


def finish(blocks, shape):
    return pl.pallas_call(
        finish_kernel,
        out_shape=jax.ShapeDtypeStruct(shape, F32),
        in_specs=[VMEM],
        out_specs=VMEM,
        compiler_params=PARAMS,
        name="finish",
    )(blocks)


def exchange(blocks, axes, count):
    shaped = blocks.reshape(count, blocks.shape[0] // count, LANES)
    return lax.all_to_all(shaped, axes, 0, 0, tiled=True).reshape(blocks.shape)


def on_device(response, direct, onset):
    groups, pairs = lax.axis_size("freq"), lax.axis_size("pair")
    rounded, own_bins, inverse, forward = (jnp.asarray(table) for table in tables())
    other_core = functools.partial(lax.ppermute, axis_name="core", perm=[(0, 1), (1, 0)])
    partners = [(owner, owner ^ (OWNERS // 2)) for owner in range(OWNERS)]
    shifted = [prepare(direct)]
    for shift in range(1, pairs):
        perm = [(pair, (pair + shift) % pairs) for pair in range(pairs)]
        shifted.append(lax.ppermute(shifted[0], "pair", perm))
    held, turned, sent = hold(direct, response)
    mine = order(shifted, held)
    other = other_core(mine)
    for step in range(ITERS):
        if step == 0:
            upgoing = far_direct(other, near_direct(mine, turned), sent, turned)
        else:
            upgoing = far_forward(other, near_forward(mine, turned), turned)
        upgoing = exchange(upgoing, "freq", groups)
        mine, other, *owned = minus_roundtrip(rounded, own_bins, onset, upgoing, step == 0)
        if step == 0:
            (direct_columns,) = owned
        other = lax.ppermute(other, "freq", partners)
        partial = first_half(mine, held)
        far = far_half(other, partial, held)
        last = step + 1 == ITERS
        near, *minus = near_half(mine, other, partial, held, last)
        partial = exchange(add(near, other_core(far)), ("pair", "freq"), pairs * groups)
        copies, dtype = (1, F32) if last else (pairs, BF16)
        plus = plus_roundtrip(inverse, forward, onset, partial, direct_columns, copies, dtype)
        if last:
            plus = finish(exchange(plus, "freq", groups), direct.shape)
        else:
            mine = exchange(plus, ("pair", "freq"), pairs * groups)
            other = other_core(mine)
    return (minus[0], plus)


def solution(mesh):
    groups, tiles = mesh.devices.shape
    devices = mesh.devices.reshape(groups, tiles // 2, 2)
    tile = ("pair", "core")
    return jax.shard_map(
        on_device,
        mesh=jax.sharding.Mesh(devices, ("freq",) + tile),
        in_specs=(P(None, "freq", tile, None), P(None, "freq", None, tile), P(None, tile)),
        out_specs=(P(None, "freq", None, tile), P(None, "freq", None, tile)),
        check_vma=False,
    )
```

```python
import functools
import math

import jax
import jax.numpy as jnp
import numpy as np
from jax import lax
from jax.experimental import pallas as pl
from jax.experimental.pallas import tpu as pltpu
from jax.sharding import PartitionSpec as P

NT = 512
ITERS = 2
FIRST_BIN = 16
NF = 128
FP = 8
LAGS = 224
LANES = 128
BF16 = jnp.bfloat16
F32 = jnp.float32
VMEM_LIMIT = 10 * 1024 * 1024

SHARED = 64
PIECES = 16
OWNERS = 32


def split(table):
    high = table.astype(np.float32).astype(jnp.bfloat16)
    low = (table - high.astype(np.float64)).astype(np.float32).astype(jnp.bfloat16)
    return high, low


def tables():
    bins = FIRST_BIN + np.arange(NF)
    lags = np.arange(LAGS)
    angle = 2.0 * math.pi / NT * ((lags[:, None] * bins[None, :]) % NT)
    weight = np.where(lags == 0, 2.0 / NT, 4.0 / NT)
    rounded, inverse, forward, own = [], [], [], []
    devices = np.arange(OWNERS)
    pair = np.stack([devices, devices ^ (OWNERS // 2)], axis=1)
    for table in (np.cos(angle), np.sin(angle)):
        high, low = split(table)
        rounded.append(np.concatenate([high, low], axis=1))
        inverse.append(np.concatenate([high, high, low], axis=1))
        high, low = split((table * weight[:, None]).T)
        forward.append(np.concatenate([high, high, low], axis=1))
        high, low = (piece.reshape(OWNERS, 4, LAGS)[pair].reshape(OWNERS, 8, LAGS) for piece in (high, low))
        rows = np.concatenate(
            [np.concatenate([high, high], axis=2), np.concatenate([low, np.zeros_like(low)], axis=2)], axis=1
        )
        own.append(rows)
    return np.stack(rounded), np.stack(own, axis=1), np.stack(inverse), np.stack(forward)


def high_low(value):
    high = value.astype(BF16)
    return high, (value - high.astype(F32)).astype(BF16)


def pieces(value):
    high, low = high_low(value)
    return jnp.concatenate([high, low, high], axis=0)


def in_vmem(array):
    return pltpu.with_memory_space_constraint(array, pltpu.VMEM)


def in_hbm(array):
    return pltpu.with_memory_space_constraint(array, pltpu.HBM)


VMEM = pl.BlockSpec(memory_space=pltpu.VMEM)
HBM = pl.BlockSpec(memory_space=pltpu.HBM)
PARAMS = pltpu.CompilerParams(vmem_limit_bytes=VMEM_LIMIT)


def hold_kernel(direct, response, kept, turned, pieces, near, held, done, near_done):
    blocks = [
        (part, bin_, slice(half * LANES, (half + 1) * LANES))
        for bin_ in range(response.shape[1])
        for part in range(2)
        for half in range(2)
    ]
    copies = [
        pltpu.make_async_copy(response.at[block], kept.at[block], done.at[step]) for step, block in enumerate(blocks)
    ]
    ahead = 6
    fetch = pltpu.make_async_copy(direct, near, near_done)
    copies[0].start()
    fetch.start()
    for copy in copies[1:ahead]:
        copy.start()
    fetch.wait()
    spread_direct(near, held, pieces)
    for step, copy in enumerate(copies):
        copy.wait()
        for later in copies[step + ahead : step + ahead + 1]:
            later.start()
        part, bin_, rows = blocks[step]
        turned[part, bin_, :, rows] = kept[part, bin_, rows, :].T


def hold(direct, response):
    parts, bins, receivers, sources = response.shape
    return pl.pallas_call(
        hold_kernel,
        out_shape=(
            pltpu.VMEM(response.shape, response.dtype),
            pltpu.VMEM((parts, bins, sources, receivers), response.dtype),
            jax.ShapeDtypeStruct((OWNERS * PIECES, LANES), BF16),
        ),
        in_specs=[HBM, HBM],
        out_specs=(VMEM, VMEM, VMEM),
        scratch_shapes=[
            pltpu.VMEM(direct.shape, F32),
            pltpu.VMEM((OWNERS * PIECES, LANES), F32),
            pltpu.SemaphoreType.DMA((2 * parts * bins,)),
            pltpu.SemaphoreType.DMA,
        ],
        compiler_params=PARAMS,
        cost_estimate=pl.CostEstimate(flops=0, bytes_accessed=4 * response.size, transcendentals=0),
        name="hold",
    )(in_hbm(direct), in_hbm(response))


def prepare_kernel(direct, out):
    for bin_ in range(direct.shape[1]):
        out[bin_] = jnp.concatenate([direct[0, bin_], direct[1, bin_]], axis=0).astype(BF16)


def prepare(direct):
    parts, bins, focal, positions = direct.shape
    return pl.pallas_call(
        prepare_kernel,
        out_shape=jax.ShapeDtypeStruct((bins, parts * focal, positions), BF16),
        in_specs=[VMEM],
        out_specs=VMEM,
        compiler_params=PARAMS,
        name="prepare",
    )(direct)


def order_kernel(*refs):
    *shifted, _, out = refs
    pairs = len(shifted)
    for shift in range(pairs):
        out[(lax.axis_index("pair") - shift + pairs) & (pairs - 1)] = shifted[shift][...]


def order(shifted, held):
    return pl.pallas_call(
        order_kernel,
        out_shape=jax.ShapeDtypeStruct((len(shifted),) + shifted[0].shape, BF16),
        in_specs=[VMEM] * (len(shifted) + 1),
        out_specs=VMEM,
        compiler_params=PARAMS,
        name="order",
    )(*shifted, in_vmem(held))


def forward_dots(blocks, turned, bin_, core):
    first = second = 0.0
    for pair, block in enumerate(blocks):
        width = block.shape[1]
        rows = pl.ds(pl.multiple_of((2 * pair + core) * width, width), width)
        first += jnp.dot(block, turned[0, bin_, rows, :], preferred_element_type=F32)
        second += jnp.dot(block, turned[1, bin_, rows, :], preferred_element_type=F32)
    return jnp.concatenate([first[:FP] - second[FP:], first[FP:] + second[:FP]], axis=0)


def share(value, bin_, out, stride):
    value = value.astype(BF16)
    for owner in range(OWNERS):
        half = owner // (OWNERS // 2)
        start = owner * stride + bin_ * 16
        out[start : start + 16, :] = value[:, half * LANES : (half + 1) * LANES]


def spread_direct(direct, held, out):
    held[...] = jnp.zeros_like(held)
    for bin_ in range(direct.shape[1]):
        for half in range(2):
            for part in range(2):
                value = direct[part, bin_, :, half * LANES : (half + 1) * LANES]
                start = (half * 2 + part) * PIECES + bin_
                for row, piece in enumerate(high_low(value)):
                    held[pl.ds(start + 4 * row, FP, stride=4 * PIECES), :] = piece.astype(F32)
    out[...] = held[...].astype(BF16)


def near_direct_kernel(mine, turned, out):
    pairs, bins = mine.shape[:2]
    core = lax.axis_index("core")
    for bin_ in range(bins):
        out[bin_] = forward_dots([mine[pair, bin_] for pair in range(pairs)], turned, bin_, core)


def near_direct(mine, turned):
    bins, _, receivers = turned.shape[1:]
    return pl.pallas_call(
        near_direct_kernel,
        out_shape=jax.ShapeDtypeStruct((bins, 2 * FP, receivers), F32),
        in_specs=[VMEM] * 2,
        out_specs=VMEM,
        compiler_params=PARAMS,
        name="near_direct",
    )(mine, in_vmem(turned))


def far_direct_kernel(other, near, pieces, turned, out):
    stride = SHARED + PIECES
    for owner in range(OWNERS):
        start = owner * stride + SHARED
        out[start : start + PIECES, :] = pieces[owner * PIECES : (owner + 1) * PIECES, :]
    pairs, bins = other.shape[:2]
    core = 1 - lax.axis_index("core")
    for bin_ in range(bins):
        value = forward_dots([other[pair, bin_] for pair in range(pairs)], turned, bin_, core)
        share(near[bin_] + value, bin_, out, stride)


def far_direct(other, near, pieces, turned):
    return pl.pallas_call(
        far_direct_kernel,
        out_shape=jax.ShapeDtypeStruct((OWNERS * (SHARED + PIECES), LANES), BF16),
        in_specs=[VMEM] * 4,
        out_specs=VMEM,
        compiler_params=PARAMS,
        name="far_direct",
    )(other, near, pieces, in_vmem(turned))


def columns_of(held, bin_):
    blocks = []
    for pair in range(held.shape[0] // NF):
        halves = []
        for half in range(2):
            start = pair * NF + half * 8 + bin_
            both = [held[pl.ds(start + part * 4, FP, stride=16), :] for part in range(2)]
            halves.append(jnp.concatenate(both, axis=0))
        blocks.append(jnp.concatenate(halves, axis=1).astype(BF16))
    return blocks


def near_forward_kernel(mine, turned, out, held):
    held[...] = mine[...].astype(F32)
    core = lax.axis_index("core")
    for bin_ in range(turned.shape[1]):
        out[bin_] = forward_dots(columns_of(held, bin_), turned, bin_, core)


def near_forward(mine, turned):
    bins, _, receivers = turned.shape[1:]
    return pl.pallas_call(
        near_forward_kernel,
        out_shape=jax.ShapeDtypeStruct((bins, 2 * FP, receivers), F32),
        in_specs=[VMEM] * 2,
        out_specs=VMEM,
        scratch_shapes=[pltpu.VMEM(mine.shape, F32)],
        compiler_params=PARAMS,
        name="near_forward",
    )(mine, in_vmem(turned))


def far_forward_kernel(other, near, turned, out, held):
    held[...] = other[...].astype(F32)
    core = 1 - lax.axis_index("core")
    for bin_ in range(turned.shape[1]):
        value = forward_dots(columns_of(held, bin_), turned, bin_, core)
        share(near[bin_] + value, bin_, out, SHARED)


def far_forward(other, near, turned):
    return pl.pallas_call(
        far_forward_kernel,
        out_shape=jax.ShapeDtypeStruct((OWNERS * SHARED, LANES), BF16),
        in_specs=[VMEM] * 3,
        out_specs=VMEM,
        scratch_shapes=[pltpu.VMEM(other.shape, F32)],
        compiler_params=PARAMS,
        name="far_forward",
    )(other, near, in_vmem(turned))


def minus_kernel(stride, rounded, own, onset, blocks, mine, other, *refs):
    *owned, spectra = refs
    for owner in range(OWNERS):
        start = owner * stride
        spectra[owner * SHARED : (owner + 1) * SHARED, :] = blocks[start : start + SHARED, :].astype(F32)
    device = lax.axis_index("freq")
    limits = jnp.where(device < OWNERS // 2, onset[:, :LANES], onset[:, LANES:])
    wide = 2
    for part in range(2):
        for focal in range(0, FP, wide):
            first = part * FP + focal
            spectrum = jnp.concatenate(
                [spectra[pl.ds(first + i, NF, stride=16), :].astype(BF16) for i in range(wide)], axis=1
            )
            spectrum = jnp.concatenate([spectrum, spectrum], axis=0)
            signal = jnp.dot(rounded[part], spectrum, preferred_element_type=F32)
            limit = jnp.concatenate([limits[focal + i : focal + i + 1, :] for i in range(wide)], axis=1)
            lag = lax.broadcasted_iota(jnp.int32, signal.shape, 0)
            signal = jnp.where(lag < limit, signal, 0.0)
            signal = jnp.concatenate(high_low(signal), axis=0)
            result = jnp.dot(own[device, part], signal, preferred_element_type=F32)
            result = result[:8] + result[8:]
            for i in range(wide):
                block = result[:, i * LANES : (i + 1) * LANES]
                mine[pl.ds(first + i, 4, stride=16), :] = block[:4]
                other[pl.ds(first + i, 4, stride=16), :] = block[4:]
    if owned:
        (owned,) = owned
        for owner in range(OWNERS):
            start = owner * stride + SHARED
            spectra[owner * PIECES : (owner + 1) * PIECES, :] = blocks[start : start + PIECES, :].astype(F32)
        for bin_ in range(4):
            high, low = (spectra[pl.ds(bin_ + 4 * i, OWNERS, stride=PIECES), :] for i in range(2))
            owned[pl.ds(bin_, OWNERS, stride=4), :] = high + low


def minus_roundtrip(rounded, own, onset, blocks, carried):
    stride = SHARED + PIECES if carried else SHARED
    out_shape = [jax.ShapeDtypeStruct((SHARED, LANES), F32)] * 2
    if carried:
        out_shape.append(jax.ShapeDtypeStruct((NF, LANES), F32))
    return pl.pallas_call(
        functools.partial(minus_kernel, stride),
        out_shape=out_shape,
        in_specs=[VMEM] * 4,
        out_specs=[VMEM] * len(out_shape),
        scratch_shapes=[pltpu.VMEM((OWNERS * SHARED, LANES), F32)],
        compiler_params=PARAMS,
        name="minus_roundtrip",
    )(rounded, own, onset, blocks)


def adjoint_dots(block, response, bin_, half, core, held, start):
    receivers, sources = response.shape[2:]
    rows = pl.ds(pl.multiple_of(half * LANES, LANES), LANES)
    width = 2 * LANES
    for pair in range(sources // (2 * width)):
        lanes = pl.ds(pl.multiple_of((2 * pair + core) * width, width), width)
        first = jnp.dot(block, response[0, bin_, rows, lanes], preferred_element_type=F32)
        second = jnp.dot(block, response[1, bin_, rows, lanes], preferred_element_type=F32)
        parts = (first[:FP] + second[FP:], first[FP:] - second[:FP])
        for side in range(2):
            for part in range(2):
                row = start + pair * NF + (side * 2 + part) * 4 + bin_
                held[pl.ds(row, FP, stride=16), :] = parts[part][:, side * LANES : (side + 1) * LANES]


def first_half_kernel(mine, response, out):
    half = lax.axis_index("freq") >> 4
    core = lax.axis_index("core")
    for bin_ in range(response.shape[1]):
        block = mine[bin_ * 16 : (bin_ + 1) * 16, :].astype(BF16)
        adjoint_dots(block, response, bin_, half, core, out, 0)
        adjoint_dots(block, response, bin_, half, 1 - core, out, out.shape[0] // 2)


def first_half(mine, response):
    rows = NF * response.shape[3] // (2 * LANES)
    return pl.pallas_call(
        first_half_kernel,
        out_shape=jax.ShapeDtypeStruct((rows, LANES), F32),
        in_specs=[VMEM] * 2,
        out_specs=VMEM,
        compiler_params=PARAMS,
        name="first_half",
    )(mine, in_vmem(response))


def far_half_kernel(other, partial, response, out, held):
    half = 1 - (lax.axis_index("freq") >> 4)
    core = 1 - lax.axis_index("core")
    for bin_ in range(response.shape[1]):
        block = other[bin_ * 16 : (bin_ + 1) * 16, :].astype(BF16)
        adjoint_dots(block, response, bin_, half, core, held, 0)
    out[...] = (held[...] + partial[held.shape[0] :, :]).astype(out.dtype)


def far_half(other, partial, response):
    rows = partial.shape[0] // 2
    return pl.pallas_call(
        far_half_kernel,
        out_shape=jax.ShapeDtypeStruct((rows, LANES), BF16),
        in_specs=[VMEM] * 3,
        out_specs=VMEM,
        scratch_shapes=[pltpu.VMEM((rows, LANES), F32)],
        compiler_params=PARAMS,
        name="far_half",
    )(other, partial, in_vmem(response))


def near_half_kernel(mine, other, partial, response, out, *refs):
    *minus, held = refs
    half = lax.axis_index("freq") >> 4
    core = lax.axis_index("core")
    for bin_ in range(response.shape[1]):
        block = other[bin_ * 16 : (bin_ + 1) * 16, :].astype(BF16)
        adjoint_dots(block, response, bin_, 1 - half, core, held, 0)
        for part in range(2):
            rows = slice(bin_ * 16 + part * FP, bin_ * 16 + (part + 1) * FP)
            for place, source in ((half, mine), (1 - half, other)):
                lanes = pl.ds(pl.multiple_of(place * LANES, LANES), LANES)
                for spectrum in minus:
                    spectrum[part, bin_, :, lanes] = source[rows, :]
    out[...] = held[...] + partial[: held.shape[0], :]


def near_half(mine, other, partial, response, last):
    rows = partial.shape[0] // 2
    out_shape = [jax.ShapeDtypeStruct((rows, LANES), F32)]
    if last:
        out_shape.append(jax.ShapeDtypeStruct((2, response.shape[1], FP, response.shape[2]), F32))
    return pl.pallas_call(
        near_half_kernel,
        out_shape=out_shape,
        in_specs=[VMEM] * 4,
        out_specs=[VMEM] * len(out_shape),
        scratch_shapes=[pltpu.VMEM((rows, LANES), F32)],
        compiler_params=PARAMS,
        name="near_half",
    )(mine, other, partial, in_vmem(response))


def add_kernel(near, far, out):
    out[...] = (near[...] + far[...].astype(F32)).astype(out.dtype)


def add(near, far):
    return pl.pallas_call(
        add_kernel,
        out_shape=jax.ShapeDtypeStruct(near.shape, BF16),
        in_specs=[VMEM, VMEM],
        out_specs=VMEM,
        compiler_params=PARAMS,
        name="add",
    )(near, far)


def plus_kernel(inverse, forward, onset, blocks, direct, out):
    device = lax.axis_index("freq")
    part, own_half, own_focal = device & 1, (device >> 1) & 1, device >> 2
    spectrum = blocks[:NF, :].astype(F32)
    for tile in range(1, blocks.shape[0] // NF):
        spectrum += blocks[tile * NF : (tile + 1) * NF, :].astype(F32)
    signal = jnp.dot(inverse[part], pieces(spectrum), preferred_element_type=F32)
    limits = jnp.where(own_half == 0, onset[:, :LANES], onset[:, LANES:])
    focal = lax.broadcasted_iota(jnp.int32, limits.shape, 0)
    limit = jnp.sum(jnp.where(focal == own_focal, limits, 0), axis=0, keepdims=True)
    lag = lax.broadcasted_iota(jnp.int32, signal.shape, 0)
    signal = jnp.where(lag < limit, signal, 0.0)
    result = jnp.dot(forward[part], pieces(signal), preferred_element_type=F32)
    result = (direct[...] + result).astype(out.dtype)
    for copy in range(out.shape[0] // NF):
        out[copy * NF : (copy + 1) * NF, :] = result


def plus_roundtrip(inverse, forward, onset, blocks, direct, copies, dtype):
    return pl.pallas_call(
        plus_kernel,
        out_shape=jax.ShapeDtypeStruct((copies * NF, LANES), dtype),
        in_specs=[VMEM] * 5,
        out_specs=VMEM,
        compiler_params=PARAMS,
        name="plus_roundtrip",
    )(inverse, forward, onset, blocks, direct)


def finish_kernel(blocks, out):
    for bin_ in range(out.shape[1]):
        for part in range(2):
            for half in range(2):
                value = blocks[pl.ds((half * 2 + part) * 4 + bin_, FP, stride=16), :]
                out[part, bin_, :, half * LANES : (half + 1) * LANES] = value


def finish(blocks, shape):
    return pl.pallas_call(
        finish_kernel,
        out_shape=jax.ShapeDtypeStruct(shape, F32),
        in_specs=[VMEM],
        out_specs=VMEM,
        compiler_params=PARAMS,
        name="finish",
    )(blocks)


def exchange(blocks, axes, count):
    shaped = blocks.reshape(count, blocks.shape[0] // count, LANES)
    return lax.all_to_all(shaped, axes, 0, 0, tiled=True).reshape(blocks.shape)


def on_device(response, direct, onset):
    groups, pairs = lax.axis_size("freq"), lax.axis_size("pair")
    rounded, own_bins, inverse, forward = (jnp.asarray(table) for table in tables())
    other_core = functools.partial(lax.ppermute, axis_name="core", perm=[(0, 1), (1, 0)])
    partners = [(owner, owner ^ (OWNERS // 2)) for owner in range(OWNERS)]
    shifted = [prepare(direct)] * pairs
    for shift in (2, 3, 1):
        perm = [(pair, (pair + shift) % pairs) for pair in range(pairs)]
        shifted[shift] = lax.ppermute(shifted[0], "pair", perm)
    held, turned, sent = hold(direct, response)
    mine = order(shifted, held)
    other = other_core(mine)
    for step in range(ITERS):
        if step == 0:
            upgoing = far_direct(other, near_direct(mine, turned), sent, turned)
        else:
            upgoing = far_forward(other, near_forward(mine, turned), turned)
        upgoing = exchange(upgoing, "freq", groups)
        mine, other, *owned = minus_roundtrip(rounded, own_bins, onset, upgoing, step == 0)
        if step == 0:
            (direct_columns,) = owned
        other = lax.ppermute(other, "freq", partners)
        partial = first_half(mine, held)
        far = far_half(other, partial, held)
        last = step + 1 == ITERS
        near, *minus = near_half(mine, other, partial, held, last)
        partial = exchange(add(near, other_core(far)), ("pair", "freq"), pairs * groups)
        copies, dtype = (1, F32) if last else (pairs, BF16)
        plus = plus_roundtrip(inverse, forward, onset, partial, direct_columns, copies, dtype)
        if last:
            plus = finish(exchange(plus, "freq", groups), direct.shape)
        else:
            mine = exchange(plus, ("pair", "freq"), pairs * groups)
            other = other_core(mine)
    return (minus[0], plus)


def solution(mesh):
    groups, tiles = mesh.devices.shape
    devices = mesh.devices.reshape(groups, tiles // 2, 2)
    tile = ("pair", "core")
    return jax.shard_map(
        on_device,
        mesh=jax.sharding.Mesh(devices, ("freq",) + tile),
        in_specs=(P(None, "freq", tile, None), P(None, "freq", None, tile), P(None, tile)),
        out_specs=(P(None, "freq", None, tile), P(None, "freq", None, tile)),
        check_vma=False,
    )
```
